512 devices in a mesh: fsdp: 64 (over y, z), tp: 8 (over x, core).
Axes of the slice: x: 4, y: 8, z: 8, core: 2. Of those that a mesh axis runs over, the one named last changes fastest.
Arguments:
- momentum: bfloat16 [8192, 28672], P('fsdp', 'tp'), may hold values from -6 to 6
- gradient: bfloat16 [8192, 28672], P('fsdp', 'tp'), may hold values from -6 to 6
- basis_rows: bfloat16 [256, 28672], P('fsdp', 'tp'), may hold values from -0.03125 to 0.03125
Outputs:
- new_momentum: bfloat16 [8192, 28672], P('fsdp', 'tp')
- new_basis: bfloat16 [256, 28672], P('fsdp', 'tp')
- update: bfloat16 [8192, 28672], P('fsdp', 'tp')
The draws below stay inside these ranges and needn't reach their ends.
All inputs are finite; a program needn't handle non-finite values.
Results may differ from the reference program's by a relative error of at most 0.017.
Values may be sent and summed in bfloat16 or wider, within the bound.
A program may use at most 64 MiB of HBM per device.

```python
import math
import jax
import jax.numpy as jnp
from jax import lax

D = 8192
FF = 28672
RANK = 256


def steps_of(own_key, shape, cuts, low, largest):
    def one(position, blocks):
        heights = jax.random.uniform(jax.random.fold_in(jax.random.fold_in(own_key, 6), position), (blocks,), jnp.float32, low / len(cuts), largest / len(cuts))
        return jnp.repeat(jnp.exp(heights), shape[position] // blocks).reshape((-1,) + (1,) * (len(shape) - position - 1))

    level = one(*cuts[0])
    for cut in cuts[1:]:
        level = level * one(*cut)
    return level


def bell_draw(stream_key, shape, deviation, reach, cuts=(), kind=jnp.bfloat16):
    level = steps_of(stream_key, shape, cuts, -0.22, 0.18) if cuts else 1.0
    result = jax.random.normal(stream_key, shape, jnp.float32) * deviation * level
    return jnp.minimum(jnp.maximum(result, -reach), reach).astype(kind)


def setup_inputs(seed: int = 0) -> dict:
    keys = jax.random.split(jax.random.key(seed), 4)
    return {
        "momentum": bell_draw(keys[0], (D, FF), 1.0, 6.0, ((0, 64), (1, 8))),
        "gradient": bell_draw(keys[1], (D, FF), 1.0, 6.0, ((0, 64), (1, 8))),
        "basis_rows": bell_draw(keys[2], (RANK, FF), FF ** -0.5, 0.03125, ((0, 64), (1, 8))),
    }


epsilon = 1e-06
momentum_decay = 0.95

def reference(momentum, gradient, basis_rows):
    buffer = (momentum.astype(jnp.float32) + gradient.astype(jnp.float32)).astype(jnp.bfloat16)
    projected = jnp.dot(buffer.astype(jnp.float32), basis_rows.T.astype(jnp.float32), preferred_element_type=jnp.float32)
    gram_matrix = jnp.dot(projected.T, projected, precision=lax.Precision.HIGHEST)
    lower_factor = jnp.linalg.cholesky(gram_matrix)
    orthonormal = lax.linalg.triangular_solve(lower_factor, projected, left_side=False, lower=True, transpose_a=True)
    ortho_low = orthonormal.astype(jnp.bfloat16)
    back_factor = jnp.dot(ortho_low.T.astype(jnp.float32), buffer.astype(jnp.float32), preferred_element_type=jnp.float32)
    column_squares = lax.optimization_barrier(jnp.sum(back_factor * back_factor, axis=1))
    new_basis = (back_factor * lax.rsqrt(column_squares + epsilon)[:, None]).astype(jnp.bfloat16)
    row_scale = jnp.sqrt(column_squares + epsilon).astype(jnp.bfloat16)
    scaled_ortho = (ortho_low.astype(jnp.float32) * row_scale.astype(jnp.float32)[None, :]).astype(jnp.bfloat16)
    new_momentum = (buffer.astype(jnp.float32) - (1.0 - momentum_decay) * jnp.dot(scaled_ortho.astype(jnp.float32), new_basis.astype(jnp.float32), preferred_element_type=jnp.float32)).astype(jnp.bfloat16)
    unit_scale = math.sqrt(D * FF / RANK)
    update = (unit_scale * jnp.dot(ortho_low.astype(jnp.float32), new_basis.astype(jnp.float32), preferred_element_type=jnp.float32)).astype(jnp.bfloat16)
    return (new_momentum, new_basis, update)
```

```python
import functools
import math

import jax
import jax.numpy as jnp
from jax import lax
from jax.experimental import pallas as pl
from jax.experimental.pallas import tpu as pltpu
from jax.sharding import PartitionSpec as P

D = 8192
FF = 28672
RANK = 256
NY = 8
NZ = 8
NF = 64
NT = 8
ROWS = D // NF
COLS = FF // NT
OWN = RANK // NF
PARTS = 4
PC = COLS // PARTS
SLOT = 16

epsilon = 1e-06
momentum_decay = 0.95
UNIT = math.sqrt(D * FF / RANK)

F32 = jnp.float32
BF16 = jnp.bfloat16
MESH = pl.DeviceIdType.MESH
HIGHEST = lax.Precision.HIGHEST


def mod8(v):
    return lax.rem(v + 16, 8)


def place():
    f = lax.axis_index("fsdp")
    t = lax.axis_index("tp")
    y = f // NZ
    z = lax.rem(f, NZ)
    even = lax.rem(y + z, 2) == 0
    return f, t, y, z, even


def line(even, y, z, k):
    along_y = jnp.where(even, k, 0)
    along_z = jnp.where(even, 0, k)
    return mod8(y + along_y) * NZ + mod8(z + along_z)


def own_slot(even, y, z):
    return jnp.where(even, z * 4 + y // 2, 32 + y * 4 + z // 2)


def rows_of(slot, count=1):
    return pl.ds(pl.multiple_of(slot * SLOT, SLOT), count * SLOT)


def greet(f, t, y, z):
    barrier = pltpu.get_barrier_semaphore()
    for k in range(1, 8):
        pl.semaphore_signal(barrier, inc=1, device_id=(mod8(y + k) * NZ + z, t), device_id_type=MESH)
        pl.semaphore_signal(barrier, inc=1, device_id=(y * NZ + mod8(z + k), t), device_id_type=MESH)
        pl.semaphore_signal(barrier, inc=1, device_id=(f, mod8(t + k)), device_id_type=MESH)
    pl.semaphore_wait(barrier, 21)


def hops_of(d, c):
    return 4 if d == c else 3


STREAMS = [(ax, d, c) for c in range(2) for ax in range(2) for d in range(2)]


def chunk(ax, origin, c):
    return rows_of(ax * 32 + origin * 4 + c * 2, 2)


def gather(buf, f, t, y, z, even, s1, r1, s2, r2):
    me = own_slot(even, y, z)
    here = jnp.where(even, y // 2, 4 + z // 2)
    for k in (4, 3, 5, 2, 6, 1, 7):
        pltpu.make_async_remote_copy(
            src_ref=buf.at[rows_of(me)],
            dst_ref=buf.at[rows_of(me)],
            send_sem=s1.at[k],
            recv_sem=r1.at[here],
            device_id=(line(even, y, z, k), t),
            device_id_type=MESH,
        ).start()

    def arrival(ax, i):
        slot = jnp.where(ax == 0, z * 4 + i, 32 + y * 4 + i)

        @pl.when(slot != me)
        def _():
            pltpu.make_async_remote_copy(
                src_ref=buf.at[rows_of(slot)],
                dst_ref=buf.at[rows_of(slot)],
                send_sem=s1.at[0],
                recv_sem=r1.at[ax * 4 + i],
                device_id=(f, mod8(t + 1)),
                device_id_type=MESH,
            ).wait_recv()

    def hop(ax, d, c, h):
        step = 1 if d == 0 else -1
        pos = z if ax == 0 else y
        origin = mod8(pos - step * h)
        to = (y * NZ + mod8(z + step)) if ax == 0 else (mod8(y + step) * NZ + z)
        return pltpu.make_async_remote_copy(
            src_ref=buf.at[chunk(ax, origin, c)],
            dst_ref=buf.at[chunk(ax, origin, c)],
            send_sem=s2.at[ax, d, c, h],
            recv_sem=r2.at[ax, d, c, h],
            device_id=(to, t),
            device_id_type=MESH,
        )

    def landed(ax, d, c, h):
        step = 1 if d == 0 else -1
        pos = z if ax == 0 else y
        origin = mod8(pos - step * (h + 1))
        pltpu.make_async_remote_copy(
            src_ref=buf.at[chunk(ax, origin, c)],
            dst_ref=buf.at[chunk(ax, origin, c)],
            send_sem=s2.at[ax, d, c, h],
            recv_sem=r2.at[ax, d, c, h],
            device_id=(f, mod8(t + 1)),
            device_id_type=MESH,
        ).wait_recv()

    sent = []
    for c in range(2):
        for ax in range(2):
            for i in (2 * c, 2 * c + 1):
                arrival(ax, i)
            for d in range(2):
                copy = hop(ax, d, c, 0)
                copy.start()
                sent.append(copy)
    for h in range(4):
        for ax, d, c in STREAMS:
            if h < hops_of(d, c):
                landed(ax, d, c, h)
                if h + 1 < hops_of(d, c):
                    copy = hop(ax, d, c, h + 1)
                    copy.start()
                    sent.append(copy)

    def finish():
        for k in range(1, 8):
            pltpu.make_async_remote_copy(
                src_ref=buf.at[rows_of(me)],
                dst_ref=buf.at[rows_of(me)],
                send_sem=s1.at[k],
                recv_sem=r1.at[here],
                device_id=(f, mod8(t + 1)),
                device_id_type=MESH,
            ).wait_send()
        for copy in sent:
            copy.wait_send()

    return finish


def exchange(src_of, dst_of, ids, pos, send, recv):
    copies = []
    for k in (4, 3, 5, 2, 6, 1, 7):
        p = mod8(pos + k)
        copy = pltpu.make_async_remote_copy(
            src_ref=src_of(p),
            dst_ref=dst_of(pos),
            send_sem=send.at[k],
            recv_sem=recv.at[8 - k],
            device_id=ids(p),
            device_id_type=MESH,
        )
        copy.start()
        copies.append(copy)
    return copies


def arrived(dst_of, ids, pos, send, recv):
    for k in range(1, 8):
        p = mod8(pos + k)
        pltpu.make_async_remote_copy(
            src_ref=dst_of(p),
            dst_ref=dst_of(p),
            send_sem=send.at[k],
            recv_sem=recv.at[k],
            device_id=ids(p),
            device_id_type=MESH,
        ).wait_recv()


def project_kernel(
    m_ref, g_ref, basis_ref, proj_ref, gram_ref,
    vbuf, bbuf, mbuf, gbuf, stage, sel, part, tbuf, gpart, ybuf, zbuf,
    local_sem, s1, r1, s2, r2, ps, pr, as_, ar, ys, yr, zs, zr, bs, br, ts, tr,
):
    f, t, y, z, even = place()
    me = own_slot(even, y, z)
    cm = pltpu.make_async_copy(m_ref, mbuf, local_sem.at[0])
    cg = pltpu.make_async_copy(g_ref, gbuf, local_sem.at[1])
    cb = pltpu.make_async_copy(basis_ref, stage, local_sem.at[2])
    cb.start()
    cm.start()
    cg.start()
    cb.wait()
    own = stage[...].astype(F32)
    pieces = [own[:, j * PC:(j + 1) * PC] for j in range(PARTS)]
    vbuf[rows_of(me), :] = jnp.concatenate(pieces, axis=0).astype(BF16)
    greet(f, t, y, z)
    finish = gather(vbuf, f, t, y, z, even, s1, r1, s2, r2)
    cm.wait()
    cg.wait()
    for j in range(PARTS):
        cols = slice(j * PC, (j + 1) * PC)
        bbuf[:, cols] = (mbuf[:, cols].astype(F32) + gbuf[:, cols].astype(F32)).astype(BF16)

    def choose(i, carry):
        base = pl.multiple_of(i * 128, 128)
        row = base + lax.broadcasted_iota(jnp.int32, (128, RANK), 0)
        slot = row // SLOT
        first, second = (slot // 4) % 8, slot % 4
        zf = first
        yf = 2 * second + (first % 2)
        yo = first
        zo = 2 * second + (1 - first % 2)
        dev = jnp.where(slot < 32, yf * NZ + zf, yo * NZ + zo)
        rank = dev * OWN + row % 4
        hit = rank == lax.broadcasted_iota(jnp.int32, (128, RANK), 1)
        sel[pl.ds(base, 128), :] = jnp.where(hit, 1.0, 0.0).astype(BF16)
        return carry

    lax.fori_loop(0, 8, choose, 0)

    piece_of = (lax.broadcasted_iota(jnp.int32, (ROWS, RANK), 1) // 4) % 4
    total = jnp.zeros((ROWS, RANK), F32)
    for g in range(4):
        acc = jnp.zeros((ROWS, RANK), F32)
        for j in range(PARTS):
            got = lax.dot_general(
                bbuf[:, j * PC:(j + 1) * PC], vbuf[g * 256:(g + 1) * 256, :],
                (((1,), (1,)), ((), ())), preferred_element_type=F32,
            )
            acc = jnp.where(piece_of == j, got, acc)
        a1 = acc.astype(BF16)
        rest = acc - a1.astype(F32)
        a2 = rest.astype(BF16)
        a3 = (rest - a2.astype(F32)).astype(BF16)
        pick = sel[g * 256:(g + 1) * 256, :]
        for a in (a3, a2, a1):
            total = total + jnp.dot(a, pick, preferred_element_type=F32)
    part[...] = total

    tp_id = lambda p: (f, p)
    y_id = lambda p: (p * NZ + z, t)
    z_id = lambda p: (y * NZ + p, t)

    slab = lambda p: pl.ds(pl.multiple_of(p * 16, 16), 16)
    c1 = exchange(lambda p: part.at[slab(p)], lambda p: tbuf.at[p], tp_id, t, ps, pr)
    tbuf[t] = part[slab(t), :]
    arrived(lambda p: tbuf.at[p], tp_id, t, ps, pr)
    sums = tbuf[0]
    for p in range(1, 8):
        sums = sums + tbuf[p]
    proj_ref[slab(t), :] = sums
    c2 = exchange(lambda p: proj_ref.at[slab(t)], lambda p: proj_ref.at[slab(p)], tp_id, t, as_, ar)
    arrived(lambda p: proj_ref.at[slab(p)], tp_id, t, as_, ar)

    pv = proj_ref[...]
    gpart[...] = lax.dot_general(pv, pv, (((0,), (0,)), ((), ())), precision=HIGHEST, preferred_element_type=F32)
    tile = lambda p: (
        pl.ds(pl.multiple_of(t * 32 + (p // 2) * 8, 8), 8),
        pl.ds(pl.multiple_of(lax.rem(p, 2) * 128, 128), 128),
    )
    c3 = exchange(lambda p: gpart.at[tile(p)], lambda p: ybuf.at[p], y_id, y, ys, yr)
    ybuf[y] = gpart[tile(y)]
    arrived(lambda p: ybuf.at[p], y_id, y, ys, yr)
    sums = ybuf[0]
    for p in range(1, 8):
        sums = sums + ybuf[p]
    zbuf[z] = sums
    c4 = exchange(lambda p: zbuf.at[z], lambda p: zbuf.at[p], z_id, z, zs, zr)
    arrived(lambda p: zbuf.at[p], z_id, z, zs, zr)
    sums = zbuf[0]
    for p in range(1, 8):
        sums = sums + zbuf[p]
    gram_ref[tile(y)] = sums
    c5 = exchange(lambda p: gram_ref.at[tile(y)], lambda p: gram_ref.at[tile(p)], y_id, y, bs, br)
    arrived(lambda p: gram_ref.at[tile(p)], y_id, y, bs, br)
    block = lambda p: pl.ds(pl.multiple_of(p * 32, 32), 32)
    c6 = exchange(lambda p: gram_ref.at[block(t)], lambda p: gram_ref.at[block(p)], tp_id, t, ts, tr)
    arrived(lambda p: gram_ref.at[block(p)], tp_id, t, ts, tr)
    finish()
    for copies in (c1, c2, c3, c4, c5, c6):
        for copy in copies:
            copy.wait_send()


def invert_kernel(gram_ref, x_ref, err_ref, sx):
    i = lax.broadcasted_iota(jnp.int32, (RANK, RANK), 0)
    j = lax.broadcasted_iota(jnp.int32, (RANK, RANK), 1)
    diagonal = i == j
    gram = gram_ref[...]
    on = jnp.where(diagonal, gram, 0.0)
    down = lax.rsqrt(jnp.sum(on, axis=1, keepdims=True))
    across = lax.rsqrt(jnp.sum(on, axis=0, keepdims=True))
    sx[:, :RANK] = gram * down * across
    sx[:, RANK:] = jnp.where(diagonal, down, 0.0)

    def miss():
        return jnp.max(jnp.abs(sx[:, :RANK] - jnp.where(diagonal, 1.0, 0.0)))

    def more(state):
        count, err = state
        return jnp.logical_and(count < 16, err > 1e-5)

    def step(state):
        count, _ = state
        e = sx[:, :RANK] - jnp.where(diagonal, 1.0, 0.0)
        w = jnp.where(i > j, -e, jnp.where(diagonal, 1.0 - 0.5 * e, 0.0))
        out = jnp.dot(w, sx[...], precision=HIGHEST, preferred_element_type=F32)
        sx[:, RANK:] = out[:, RANK:]
        sx[:, :RANK] = lax.dot_general(
            out[:, :RANK], w, (((1,), (1,)), ((), ())), precision=HIGHEST, preferred_element_type=F32
        )
        return count + 1, miss()

    _, err = lax.while_loop(more, step, (jnp.int32(0), miss()))
    x_ref[...] = sx[:, RANK:]
    err_ref[0] = err


def back_kernel(
    m_ref, g_ref, proj_ref, x_ref, mom_ref, own_ref, upd_ref,
    mbuf, gbuf, bbuf, wbuf, obuf, land, ring, near, far, sqbuf,
    local_sem, s1, r1, s2, r2, s3, r3, s4, r4, qs, qr,
):
    f, t, y, z, even = place()
    me = own_slot(even, y, z)
    cm = pltpu.make_async_copy(m_ref, mbuf, local_sem.at[0])
    cg = pltpu.make_async_copy(g_ref, gbuf, local_sem.at[1])
    cm.start()
    cg.start()
    ortho = lax.dot_general(
        proj_ref[...], x_ref[...], (((1,), (1,)), ((), ())), precision=HIGHEST, preferred_element_type=F32
    )
    low = ortho.astype(BF16)
    cm.wait()
    cg.wait()
    for j in range(PARTS):
        cols = slice(j * PC, (j + 1) * PC)
        b = (mbuf[:, cols].astype(F32) + gbuf[:, cols].astype(F32)).astype(BF16)
        bbuf[:, cols] = b
        wbuf[j * RANK:(j + 1) * RANK, :] = lax.dot_general(
            low, b, (((0,), (0,)), ((), ())), preferred_element_type=F32
        ).astype(BF16)
    greet(f, t, y, z)

    def hop(ax, d, c, h, src):
        step = 1 if d == 0 else -1
        to = (y * NZ + mod8(z + step)) if ax == 0 else (mod8(y + step) * NZ + z)
        return pltpu.make_async_remote_copy(
            src_ref=src,
            dst_ref=land.at[ax, d, c, h],
            send_sem=s3.at[ax, d, c, h],
            recv_sem=r3.at[ax, d, c, h],
            device_id=(to, t),
            device_id_type=MESH,
        )

    sent = []
    for ax, d, c in STREAMS:
        step = 1 if d == 0 else -1
        pos = z if ax == 0 else y
        n = hops_of(d, c)
        copy = hop(ax, d, c, 0, wbuf.at[chunk(ax, mod8(pos + step * n), c)])
        copy.start()
        sent.append(copy)
    for h in range(4):
        for ax, d, c in STREAMS:
            step = 1 if d == 0 else -1
            pos = z if ax == 0 else y
            n = hops_of(d, c)
            if h < n:
                hop(ax, d, c, h, land.at[ax, d, c, h]).wait_recv()
                if h + 1 < n:
                    mine = wbuf[chunk(ax, mod8(pos + step * (n - h - 1)), c), :]
                    ring[ax, d, c, h] = (mine.astype(F32) + land[ax, d, c, h].astype(F32)).astype(BF16)
                    copy = hop(ax, d, c, h + 1, ring.at[ax, d, c, h])
                    copy.start()
                    sent.append(copy)

    spot = jnp.where(even, y, z)
    for ax in range(2):
        pos = z if ax == 0 else y
        cross = y if ax == 0 else z
        for c in range(2):
            both = wbuf[chunk(ax, pos, c), :].astype(F32)
            for d in range(2):
                both = both + land[ax, d, c, hops_of(d, c) - 1].astype(F32)
            near[ax, c] = both.astype(BF16)
            for i in range(2):
                odd = lax.rem(pos, 2) if ax == 0 else 1 - lax.rem(pos, 2)
                to = 2 * (2 * c + i) + odd

                @pl.when(to != cross)
                def _():
                    pltpu.make_async_remote_copy(
                        src_ref=near.at[ax, c, pl.ds(i * SLOT, SLOT)],
                        dst_ref=far.at[cross],
                        send_sem=s4.at[ax, 2 * c + i],
                        recv_sem=r4.at[cross],
                        device_id=((to * NZ + z) if ax == 0 else (y * NZ + to), t),
                        device_id_type=MESH,
                    ).start()

                @pl.when(to == cross)
                def _():
                    far[cross] = near[ax, c, i * SLOT:(i + 1) * SLOT, :]

    for k in range(1, 8):
        p = mod8(spot + k)
        pltpu.make_async_remote_copy(
            src_ref=far.at[p],
            dst_ref=far.at[p],
            send_sem=s4.at[0, 0],
            recv_sem=r4.at[p],
            device_id=(f, mod8(t + 1)),
            device_id_type=MESH,
        ).wait_recv()
    sums = far[0].astype(F32)
    for p in range(1, 8):
        sums = sums + far[p].astype(F32)
    obuf[rows_of(me), :] = sums.astype(BF16)

    finish = gather(obuf, f, t, y, z, even, s1, r1, s2, r2)

    ones = jnp.ones((8, PC), BF16)
    sq = jnp.zeros((8, RANK), F32)
    for j in range(PARTS):
        v = obuf[j * RANK:(j + 1) * RANK, :].astype(F32)
        v = v * v
        hi = v.astype(BF16)
        lo = (v - hi.astype(F32)).astype(BF16)
        for a in (lo, hi):
            sq = sq + lax.dot_general(ones, a, (((1,), (1,)), ((), ())), preferred_element_type=F32)
    tp_id = lambda p: (f, p)
    sqbuf[t] = sq
    c1 = exchange(lambda p: sqbuf.at[t], lambda p: sqbuf.at[p], tp_id, t, qs, qr)
    arrived(lambda p: sqbuf.at[p], tp_id, t, qs, qr)
    squares = sqbuf[0]
    for p in range(1, 8):
        squares = squares + sqbuf[p]
    squares = squares + epsilon
    scale = jnp.sqrt(squares)[0:1, :].astype(BF16).astype(F32)
    inverse = jnp.transpose(jnp.broadcast_to(lax.rsqrt(squares)[0:1, :], (128, RANK)))[:, 0:1]
    scaled = (low.astype(F32) * scale).astype(BF16)
    pick = jnp.where(
        lax.broadcasted_iota(jnp.int32, (8, RANK), 0) + f * OWN == lax.broadcasted_iota(jnp.int32, (8, RANK), 1),
        1.0, 0.0,
    ).astype(BF16)
    for j in range(PARTS):
        cols = slice(j * PC, (j + 1) * PC)
        nb = (obuf[j * RANK:(j + 1) * RANK, :].astype(F32) * inverse).astype(BF16)
        own_ref[:, cols] = jnp.dot(pick, nb, preferred_element_type=F32)[0:OWN].astype(BF16)
        upd_ref[:, cols] = (UNIT * jnp.dot(low, nb, preferred_element_type=F32)).astype(BF16)
        mom_ref[:, cols] = (
            bbuf[:, cols].astype(F32) - (1.0 - momentum_decay) * jnp.dot(scaled, nb, preferred_element_type=F32)
        ).astype(BF16)

    finish()
    for copy in sent:
        copy.wait_send()
    for copy in c1:
        copy.wait_send()
    for ax in range(2):
        pos = z if ax == 0 else y
        cross = y if ax == 0 else z
        for c in range(2):
            for i in range(2):
                odd = lax.rem(pos, 2) if ax == 0 else 1 - lax.rem(pos, 2)
                to = 2 * (2 * c + i) + odd

                @pl.when(to != cross)
                def _():
                    pltpu.make_async_remote_copy(
                        src_ref=near.at[ax, c, pl.ds(i * SLOT, SLOT)],
                        dst_ref=far.at[cross],
                        send_sem=s4.at[ax, 2 * c + i],
                        recv_sem=r4.at[cross],
                        device_id=(f, mod8(t + 1)),
                        device_id_type=MESH,
                    ).wait_send()


VMEM = pl.BlockSpec(memory_space=pltpu.VMEM)
ANY = pl.BlockSpec(memory_space=pl.ANY)
DMA = pltpu.SemaphoreType.DMA
LIMIT = 48 * 2**20


def project(momentum, gradient, basis_rows):
    return pl.pallas_call(
        project_kernel,
        out_shape=[jax.ShapeDtypeStruct((ROWS, RANK), F32), jax.ShapeDtypeStruct((RANK, RANK), F32)],
        in_specs=[ANY, ANY, ANY],
        out_specs=[VMEM, VMEM],
        scratch_shapes=[
            pltpu.VMEM((NF * SLOT, PC), BF16),
            pltpu.VMEM((ROWS, COLS), BF16),
            pltpu.VMEM((ROWS, COLS), BF16),
            pltpu.VMEM((ROWS, COLS), BF16),
            pltpu.VMEM((OWN, COLS), BF16),
            pltpu.VMEM((NF * SLOT, RANK), BF16),
            pltpu.VMEM((ROWS, RANK), F32),
            pltpu.VMEM((8, 16, RANK), F32),
            pltpu.VMEM((RANK, RANK), F32),
            pltpu.VMEM((8, 8, 128), F32),
            pltpu.VMEM((8, 8, 128), F32),
            DMA((3,)),
            DMA((8,)), DMA((8,)), DMA((2, 2, 2, 4)), DMA((2, 2, 2, 4)),
        ] + [DMA((8,))] * 12,
        compiler_params=pltpu.CompilerParams(collective_id=0, has_side_effects=True, vmem_limit_bytes=LIMIT),
        name="project",
    )(momentum, gradient, basis_rows)


def invert(gram):
    return pl.pallas_call(
        invert_kernel,
        out_shape=[jax.ShapeDtypeStruct((RANK, RANK), F32), jax.ShapeDtypeStruct((1,), F32)],
        in_specs=[VMEM],
        out_specs=[VMEM, pl.BlockSpec(memory_space=pltpu.SMEM)],
        scratch_shapes=[pltpu.VMEM((RANK, 2 * RANK), F32)],
        compiler_params=pltpu.CompilerParams(vmem_limit_bytes=LIMIT),
        name="invert",
    )(gram)


def back(momentum, gradient, proj, x):
    return pl.pallas_call(
        back_kernel,
        out_shape=[
            jax.ShapeDtypeStruct((ROWS, COLS), BF16),
            jax.ShapeDtypeStruct((OWN, COLS), BF16),
            jax.ShapeDtypeStruct((ROWS, COLS), BF16),
        ],
        in_specs=[ANY, ANY, VMEM, VMEM],
        out_specs=[VMEM, VMEM, VMEM],
        scratch_shapes=[
            pltpu.VMEM((ROWS, COLS), BF16),
            pltpu.VMEM((ROWS, COLS), BF16),
            pltpu.VMEM((ROWS, COLS), BF16),
            pltpu.VMEM((NF * SLOT, PC), BF16),
            pltpu.VMEM((NF * SLOT, PC), BF16),
            pltpu.VMEM((2, 2, 2, 4, 2 * SLOT, PC), BF16),
            pltpu.VMEM((2, 2, 2, 3, 2 * SLOT, PC), BF16),
            pltpu.VMEM((2, 2, 2 * SLOT, PC), BF16),
            pltpu.VMEM((8, SLOT, PC), BF16),
            pltpu.VMEM((8, 8, RANK), F32),
            DMA((2,)),
            DMA((8,)), DMA((8,)), DMA((2, 2, 2, 4)), DMA((2, 2, 2, 4)),
            DMA((2, 2, 2, 4)), DMA((2, 2, 2, 4)), DMA((2, 4)), DMA((8,)), DMA((8,)), DMA((8,)),
        ],
        compiler_params=pltpu.CompilerParams(collective_id=1, has_side_effects=True, vmem_limit_bytes=LIMIT),
        name="back",
    )(momentum, gradient, proj, x)


def direct(gram):
    lower_factor = jnp.linalg.cholesky(gram)
    return lax.linalg.triangular_solve(lower_factor, jnp.eye(RANK, dtype=F32), left_side=True, lower=True)


def local(momentum, gradient, basis_rows):
    proj, gram = project(momentum, gradient, basis_rows)
    x, err = invert(gram)
    x = lax.cond(err[0] < 1e-5, lambda g, v: v, lambda g, v: direct(g), gram, x)
    return tuple(back(momentum, gradient, proj, x))


def solution(mesh):
    return jax.shard_map(
        local,
        mesh=mesh,
        in_specs=(P("fsdp", "tp"), P("fsdp", "tp"), P("fsdp", "tp")),
        out_specs=(P("fsdp", "tp"), P("fsdp", "tp"), P("fsdp", "tp")),
        check_vma=False,
    )
```

```python
import functools
import math

import jax
import jax.numpy as jnp
from jax import lax
from jax.experimental import pallas as pl
from jax.experimental.pallas import tpu as pltpu
from jax.sharding import PartitionSpec as P

D = 8192
FF = 28672
RANK = 256
NY = 8
NZ = 8
NF = 64
NT = 8
ROWS = D // NF
COLS = FF // NT
OWN = RANK // NF
PARTS = 4
PC = COLS // PARTS
SLOT = 16
CUT = COLS // NF
PAD = 64

epsilon = 1e-06
momentum_decay = 0.95
UNIT = math.sqrt(D * FF / RANK)

F32 = jnp.float32
BF16 = jnp.bfloat16
MESH = pl.DeviceIdType.MESH
HIGHEST = lax.Precision.HIGHEST


def mod8(v):
    return lax.rem(v + 16, 8)


def place():
    f = lax.axis_index("fsdp")
    t = lax.axis_index("tp")
    y = f // NZ
    z = lax.rem(f, NZ)
    even = lax.rem(y + z, 2) == 0
    return f, t, y, z, even


def line(even, y, z, k):
    along_y = jnp.where(even, k, 0)
    along_z = jnp.where(even, 0, k)
    return mod8(y + along_y) * NZ + mod8(z + along_z)


def own_slot(even, y, z):
    return jnp.where(even, z * 4 + y // 2, 32 + y * 4 + z // 2)


def greet(f, t, y, z):
    barrier = pltpu.get_barrier_semaphore()
    for k in range(1, 8):
        pl.semaphore_signal(barrier, inc=1, device_id=(mod8(y + k) * NZ + z, t), device_id_type=MESH)
        pl.semaphore_signal(barrier, inc=1, device_id=(y * NZ + mod8(z + k), t), device_id_type=MESH)
        pl.semaphore_signal(barrier, inc=1, device_id=(f, mod8(t + k)), device_id_type=MESH)
    pl.semaphore_wait(barrier, 21)


ORDER = (0, 1, 3, 2)


def fourth(d, i):
    return (i < 2) if d == 0 else (i >= 2)


def slot_of(ax, origin, i):
    return ax * 32 + origin * 4 + i


def beside(ax, d, y, z):
    step = 1 if d == 0 else -1
    return (y * NZ + mod8(z + step)) if ax == 0 else (mod8(y + step) * NZ + z)


def gather(buf, size, f, t, y, z, even, s1, r1, s2, r2, between):
    rows = lambda slot: buf.at[pl.ds(pl.multiple_of(slot * size, size), size)]
    me = own_slot(even, y, z)
    at = (z, y)
    half = (y // 2, z // 2)
    home = (even, jnp.logical_not(even))
    here = jnp.where(even, y // 2, 4 + z // 2)
    aside = (f, mod8(t + 1))

    def straight(k, to):
        return pltpu.make_async_remote_copy(
            src_ref=rows(me), dst_ref=rows(me), send_sem=s1.at[k], recv_sem=r1.at[here],
            device_id=to, device_id_type=MESH,
        )

    def copy(ax, d, i, h, origin, to):
        slot = slot_of(ax, origin, i)
        return pltpu.make_async_remote_copy(
            src_ref=rows(slot), dst_ref=rows(slot), send_sem=s2.at[ax, d, i, h], recv_sem=r2.at[ax, d, i, h],
            device_id=to, device_id_type=MESH,
        )

    def send(ax, d, i, h):
        step = 1 if d == 0 else -1
        copy(ax, d, i, h, mod8(at[ax] - step * h), (beside(ax, d, y, z), t)).start()

    def landed(ax, d, i, h):
        step = 1 if d == 0 else -1
        copy(ax, d, i, h, mod8(at[ax] - step * (h + 1)), aside).wait_recv()

    for ax in range(2):
        @pl.when(home[ax])
        def _():
            for d in range(2):
                send(ax, d, half[ax], 0)
    for k in (1, 7, 2, 6, 3, 5, 4):
        straight(k, (line(even, y, z, k), t)).start()
    between[0]()
    for r in ORDER:
        for ax in range(2):
            i = lax.rem(half[ax] + r, 4)

            def first():
                slot = slot_of(ax, at[ax], i)
                pltpu.make_async_remote_copy(
                    src_ref=rows(slot), dst_ref=rows(slot), send_sem=s1.at[0], recv_sem=r1.at[ax * 4 + i],
                    device_id=aside, device_id_type=MESH,
                ).wait_recv()
                for d in range(2):
                    send(ax, d, i, 0)

            if r == 0:
                pl.when(jnp.logical_not(home[ax]))(first)
            else:
                first()
    between[1]()
    for h in range(4):
        for r in ORDER:
            for ax in range(2):
                i = lax.rem(half[ax] + r, 4)
                for d in range(2):
                    if h < 2:
                        landed(ax, d, i, h)
                        send(ax, d, i, h + 1)
                    elif h == 2:
                        landed(ax, d, i, h)

                        @pl.when(fourth(d, i))
                        def _():
                            send(ax, d, i, 3)
                    else:

                        @pl.when(fourth(d, i))
                        def _():
                            landed(ax, d, i, 3)
        between[h + 2]()

    def finish():
        for k in range(1, 8):
            straight(k, aside).wait_send()
        for ax in range(2):
            for d in range(2):
                for i in range(4):
                    for h in range(4 if fourth(d, i) else 3):
                        copy(ax, d, i, h, at[ax], aside).wait_send()

    return finish


def exchange(src_of, dst_of, ids, pos, send, recv):
    copies = []
    for k in (4, 3, 5, 2, 6, 1, 7):
        p = mod8(pos + k)
        copy = pltpu.make_async_remote_copy(
            src_ref=src_of(p),
            dst_ref=dst_of(pos),
            send_sem=send.at[k],
            recv_sem=recv.at[8 - k],
            device_id=ids(p),
            device_id_type=MESH,
        )
        copy.start()
        copies.append(copy)
    return copies


def arrived(dst_of, ids, pos, send, recv):
    for k in range(1, 8):
        p = mod8(pos + k)
        pltpu.make_async_remote_copy(
            src_ref=dst_of(p),
            dst_ref=dst_of(p),
            send_sem=send.at[k],
            recv_sem=recv.at[k],
            device_id=ids(p),
            device_id_type=MESH,
        ).wait_recv()


def thirds(v):
    a1 = v.astype(BF16)
    rest = v - a1.astype(F32)
    a2 = rest.astype(BF16)
    return a1, a2, (rest - a2.astype(F32)).astype(BF16)


def project_kernel(
    m_ref, g_ref, basis_ref, proj_ref, gram_ref, z_ref,
    vbuf, bbuf, mbuf, gbuf, stage, sel, part, tbuf, gpart, ybuf, zbuf, work, land, near, far,
    local_sem, s1, r1, s2, r2, s3, r3, s4, r4, ps, pr, as_, ar, ys, yr, zs, zr, bs, br, ts, tr,
):
    f, t, y, z, even = place()
    me = own_slot(even, y, z)
    at = (z, y)
    aside = (f, mod8(t + 1))
    cm = pltpu.make_async_copy(m_ref, mbuf, local_sem.at[0])
    cg = pltpu.make_async_copy(g_ref, gbuf, local_sem.at[1])
    cb = pltpu.make_async_copy(basis_ref, stage, local_sem.at[2])
    cb.start()
    cm.start()
    cg.start()
    cb.wait()
    own = stage[...].astype(F32)
    pieces = [own[:, j * PC:(j + 1) * PC] for j in range(PARTS)]
    vbuf[pl.ds(pl.multiple_of(me * SLOT, SLOT), SLOT), :] = jnp.concatenate(pieces, axis=0).astype(BF16)
    greet(f, t, y, z)

    def prepare():
        cm.wait()
        cg.wait()
        for j in range(PARTS):
            cols = slice(j * PC, (j + 1) * PC)
            bbuf[:, cols] = (mbuf[:, cols].astype(F32) + gbuf[:, cols].astype(F32)).astype(BF16)
        part[...] = jnp.zeros((ROWS, RANK), F32)

        def choose(i, carry):
            base = pl.multiple_of(i * 128, 128)
            row = base + lax.broadcasted_iota(jnp.int32, (128, RANK), 0)
            slot = row // SLOT
            first, second = (slot // 4) % 8, slot % 4
            yf = 2 * second + (first % 2)
            zo = 2 * second + (1 - first % 2)
            dev = jnp.where(slot < 32, yf * NZ + first, first * NZ + zo)
            hit = dev * OWN + row % 4 == lax.broadcasted_iota(jnp.int32, (128, RANK), 1)
            sel[pl.ds(base, 128), :] = jnp.where(hit, 1.0, 0.0).astype(BF16)
            return carry

        lax.fori_loop(0, 8, choose, 0)

    def level(h):
        def run():
            if h == 0 or h == 4:
                starts = [slot_of(ax, mod8(at[ax] + h), 0) * SLOT for ax in range(2)]
            else:
                starts = [slot_of(ax, mod8(at[ax] + s), 0) * SLOT for ax in range(2) for s in (h, -h)]
            spans = [pl.ds(pl.multiple_of(s, 64), 64) for s in starts]
            v = jnp.concatenate([vbuf[s, :] for s in spans], axis=0)
            pick = jnp.concatenate([sel[s, :] for s in spans], axis=0)
            piece_of = (lax.broadcasted_iota(jnp.int32, (ROWS, v.shape[0]), 1) // 4) % 4
            acc = jnp.zeros((ROWS, v.shape[0]), F32)
            for j in range(PARTS):
                got = lax.dot_general(
                    bbuf[:, j * PC:(j + 1) * PC], v, (((1,), (1,)), ((), ())), preferred_element_type=F32
                )
                acc = jnp.where(piece_of == j, got, acc)
            total = part[...]
            for a in thirds(acc)[::-1]:
                total = total + jnp.dot(a, pick, preferred_element_type=F32)
            part[...] = total
        return run

    finish = gather(
        vbuf, SLOT, f, t, y, z, even, s1, r1, s2, r2,
        [prepare, level(0), level(1), level(2), level(3), level(4)],
    )

    tp_id = lambda p: (f, p)
    y_id = lambda p: (p * NZ + z, t)
    z_id = lambda p: (y * NZ + p, t)

    slab = lambda p: pl.ds(pl.multiple_of(p * 16, 16), 16)
    c1 = exchange(lambda p: part.at[slab(p)], lambda p: tbuf.at[p], tp_id, t, ps, pr)
    tbuf[t] = part[slab(t), :]
    arrived(lambda p: tbuf.at[p], tp_id, t, ps, pr)
    sums = tbuf[0]
    for p in range(1, 8):
        sums = sums + tbuf[p]
    proj_ref[slab(t), :] = sums
    c2 = exchange(lambda p: proj_ref.at[slab(t)], lambda p: proj_ref.at[slab(p)], tp_id, t, as_, ar)
    arrived(lambda p: proj_ref.at[slab(p)], tp_id, t, as_, ar)

    pv = proj_ref[...]
    gpart[...] = lax.dot_general(pv, pv, (((0,), (0,)), ((), ())), precision=HIGHEST, preferred_element_type=F32)
    tile = lambda p: (
        pl.ds(pl.multiple_of(t * 32 + (p // 2) * 8, 8), 8),
        pl.ds(pl.multiple_of(lax.rem(p, 2) * 128, 128), 128),
    )
    c3 = exchange(lambda p: gpart.at[tile(p)], lambda p: ybuf.at[p], y_id, y, ys, yr)
    ybuf[y] = gpart[tile(y)]

    split = thirds(pv)
    for j in range(7):
        cols = slice(j * 512, (j + 1) * 512)
        total = jnp.zeros((512, RANK), F32)
        for a in split[::-1]:
            total = total + lax.dot_general(
                bbuf[:, cols], a, (((0,), (0,)), ((), ())), preferred_element_type=F32
            )
        work[cols, :] = total
    cut = lambda ax, origin, i: pl.ds(pl.multiple_of(slot_of(ax, origin, i) * CUT, 8), CUT)
    streams = [(ax, d, i) for i in range(4) for ax in range(2) for d in range(2)]
    hops = lambda d, i: 4 if fourth(d, i) else 3
    sent = []

    def pass_on(ax, d, i, h, src):
        copy = pltpu.make_async_remote_copy(
            src_ref=src, dst_ref=land.at[ax, d, i, h], send_sem=s3.at[ax, d, i, h], recv_sem=r3.at[ax, d, i, h],
            device_id=(beside(ax, d, y, z), t), device_id_type=MESH,
        )
        copy.start()
        sent.append(copy)

    def came(ax, d, i, h):
        pltpu.make_async_remote_copy(
            src_ref=land.at[ax, d, i, h], dst_ref=land.at[ax, d, i, h], send_sem=s3.at[ax, d, i, h],
            recv_sem=r3.at[ax, d, i, h], device_id=aside, device_id_type=MESH,
        ).wait_recv()

    def ring(h):
        for ax, d, i in streams:
            n = hops(d, i)
            if h < n:
                came(ax, d, i, h)
                if h + 1 < n:
                    step = 1 if d == 0 else -1
                    land[ax, d, i, h] = land[ax, d, i, h] + work[cut(ax, mod8(at[ax] + step * (n - h - 1)), i), :]
                    pass_on(ax, d, i, h + 1, land.at[ax, d, i, h])

    for ax, d, i in streams:
        step = 1 if d == 0 else -1
        pass_on(ax, d, i, 0, work.at[cut(ax, mod8(at[ax] + step * hops(d, i)), i)])
    arrived(lambda p: ybuf.at[p], y_id, y, ys, yr)
    sums = ybuf[0]
    for p in range(1, 8):
        sums = sums + ybuf[p]
    zbuf[z] = sums
    c4 = exchange(lambda p: zbuf.at[z], lambda p: zbuf.at[p], z_id, z, zs, zr)
    ring(0)
    arrived(lambda p: zbuf.at[p], z_id, z, zs, zr)
    sums = zbuf[0]
    for p in range(1, 8):
        sums = sums + zbuf[p]
    gram_ref[tile(y)] = sums
    c5 = exchange(lambda p: gram_ref.at[tile(y)], lambda p: gram_ref.at[tile(p)], y_id, y, bs, br)
    ring(1)
    arrived(lambda p: gram_ref.at[tile(p)], y_id, y, bs, br)
    block = lambda p: pl.ds(pl.multiple_of(p * 32, 32), 32)
    c6 = exchange(lambda p: gram_ref.at[block(t)], lambda p: gram_ref.at[block(p)], tp_id, t, ts, tr)
    ring(2)
    ring(3)

    spot = jnp.where(even, y, z)

    def target(ax, i):
        odd = lax.rem(at[ax], 2) if ax == 0 else 1 - lax.rem(at[ax], 2)
        return 2 * i + odd

    def cross(ax, i, device):
        return pltpu.make_async_remote_copy(
            src_ref=near.at[ax, i], dst_ref=far.at[at[1 - ax]], send_sem=s4.at[ax, i], recv_sem=r4.at[at[1 - ax]],
            device_id=device, device_id_type=MESH,
        )

    for ax in range(2):
        for i in range(4):
            both = work[cut(ax, at[ax], i), :]
            for d in range(2):
                both = both + land[ax, d, i, hops(d, i) - 1]
            near[ax, i] = both
            to = target(ax, i)

            @pl.when(to != at[1 - ax])
            def _():
                cross(ax, i, ((to * NZ + z) if ax == 0 else (y * NZ + to), t)).start()

            @pl.when(to == at[1 - ax])
            def _():
                far[at[1 - ax]] = both

    arrived(lambda p: gram_ref.at[block(p)], tp_id, t, ts, tr)
    for k in range(1, 8):
        p = mod8(spot + k)
        pltpu.make_async_remote_copy(
            src_ref=far.at[p], dst_ref=far.at[p], send_sem=s4.at[0, 0], recv_sem=r4.at[p],
            device_id=aside, device_id_type=MESH,
        ).wait_recv()
    sums = far[0]
    for p in range(1, 8):
        sums = sums + far[p]
    z_ref[...] = sums
    finish()
    for copies in (c1, c2, c3, c4, c5, c6, sent):
        for copy in copies:
            copy.wait_send()
    for ax in range(2):
        for i in range(4):
            @pl.when(target(ax, i) != at[1 - ax])
            def _():
                cross(ax, i, aside).wait_send()


def invert_kernel(gram_ref, x_ref, err_ref, sx):
    i = lax.broadcasted_iota(jnp.int32, (RANK, RANK), 0)
    j = lax.broadcasted_iota(jnp.int32, (RANK, RANK), 1)
    diagonal = i == j
    gram = gram_ref[...]
    on = jnp.where(diagonal, gram, 0.0)
    down = lax.rsqrt(jnp.sum(on, axis=1, keepdims=True))
    across = lax.rsqrt(jnp.sum(on, axis=0, keepdims=True))
    sx[:, :RANK] = gram * down * across
    sx[:, RANK:] = jnp.where(diagonal, down, 0.0)

    def miss():
        return jnp.max(jnp.abs(sx[:, :RANK] - jnp.where(diagonal, 1.0, 0.0)))

    def more(state):
        count, err = state
        return jnp.logical_and(count < 16, err > 1e-5)

    def step(state):
        count, _ = state
        e = sx[:, :RANK] - jnp.where(diagonal, 1.0, 0.0)
        w = jnp.where(i > j, -e, jnp.where(diagonal, 1.0 - 0.5 * e, 0.0))
        out = jnp.dot(w, sx[...], precision=HIGHEST, preferred_element_type=F32)
        sx[:, RANK:] = out[:, RANK:]
        sx[:, :RANK] = lax.dot_general(
            out[:, :RANK], w, (((1,), (1,)), ((), ())), precision=HIGHEST, preferred_element_type=F32
        )
        return count + 1, miss()

    _, err = lax.while_loop(more, step, (jnp.int32(0), miss()))
    x_ref[...] = sx[:, RANK:]
    err_ref[0] = err


def back_kernel(
    m_ref, g_ref, proj_ref, x_ref, z_ref, mom_ref, own_ref, upd_ref,
    mbuf, gbuf, bbuf, obuf, qbuf, tbuf, ybuf, zbuf,
    local_sem, s1, r1, s2, r2, ts, tr, ys, yr, zs, zr,
):
    f, t, y, z, even = place()
    me = own_slot(even, y, z)
    cm = pltpu.make_async_copy(m_ref, mbuf, local_sem.at[0])
    cg = pltpu.make_async_copy(g_ref, gbuf, local_sem.at[1])
    cm.start()
    cg.start()
    tp_id = lambda p: (f, p)
    y_id = lambda p: (p * NZ + z, t)
    z_id = lambda p: (y * NZ + p, t)
    mine = lax.dot_general(
        z_ref[...], x_ref[...], (((1,), (1,)), ((), ())), precision=HIGHEST, preferred_element_type=F32
    )
    obuf[pl.ds(pl.multiple_of(me * PAD, PAD), PAD), :] = jnp.concatenate(
        [mine, jnp.zeros((PAD - CUT, RANK), F32)], axis=0
    ).astype(BF16)
    tbuf[t] = jnp.broadcast_to(jnp.sum(mine * mine, axis=0, keepdims=True), (8, RANK))
    greet(f, t, y, z)
    waits = []

    def open_squares():
        waits.extend(exchange(lambda p: tbuf.at[t], lambda p: tbuf.at[p], tp_id, t, ts, tr))
        cm.wait()
        cg.wait()
        for j in range(PARTS):
            cols = slice(j * PC, (j + 1) * PC)
            bbuf[:, cols] = (mbuf[:, cols].astype(F32) + gbuf[:, cols].astype(F32)).astype(BF16)
        qbuf[...] = lax.dot_general(
            proj_ref[...], x_ref[...], (((1,), (1,)), ((), ())), precision=HIGHEST, preferred_element_type=F32
        ).astype(BF16)

    def fold(buf):
        sums = buf[0]
        for p in range(1, 8):
            sums = sums + buf[p]
        return sums

    def over_y():
        arrived(lambda p: tbuf.at[p], tp_id, t, ts, tr)
        ybuf[y] = fold(tbuf)
        waits.extend(exchange(lambda p: ybuf.at[y], lambda p: ybuf.at[p], y_id, y, ys, yr))

    def over_z():
        arrived(lambda p: ybuf.at[p], y_id, y, ys, yr)
        zbuf[z] = fold(ybuf)
        waits.extend(exchange(lambda p: zbuf.at[z], lambda p: zbuf.at[p], z_id, z, zs, zr))

    nothing = lambda: None
    finish = gather(
        obuf, PAD, f, t, y, z, even, s1, r1, s2, r2,
        [open_squares, over_y, over_z, nothing, nothing, nothing],
    )
    arrived(lambda p: zbuf.at[p], z_id, z, zs, zr)
    squares = fold(zbuf)[0:1, :] + epsilon
    inverse = lax.rsqrt(squares)
    low = qbuf[...]
    scaled = (low.astype(F32) * jnp.sqrt(squares).astype(BF16).astype(F32)).astype(BF16)
    pick = jnp.where(
        lax.broadcasted_iota(jnp.int32, (8, RANK), 0) + f * OWN == lax.broadcasted_iota(jnp.int32, (8, RANK), 1),
        1.0, 0.0,
    ).astype(BF16)
    turn = (((1,), (1,)), ((), ()))
    for j in range(PARTS):
        cols = slice(j * PC, (j + 1) * PC)
        pieces = [obuf[s * PAD:s * PAD + CUT, :].astype(F32) for s in range(j * 16, (j + 1) * 16)]
        nb = (jnp.concatenate(pieces, axis=0) * inverse).astype(BF16)
        own_ref[:, cols] = lax.dot_general(pick, nb, turn, preferred_element_type=F32)[0:OWN].astype(BF16)
        upd_ref[:, cols] = (UNIT * lax.dot_general(low, nb, turn, preferred_element_type=F32)).astype(BF16)
        mom_ref[:, cols] = (
            bbuf[:, cols].astype(F32)
            - (1.0 - momentum_decay) * lax.dot_general(scaled, nb, turn, preferred_element_type=F32)
        ).astype(BF16)
    finish()
    for copy in waits:
        copy.wait_send()


VMEM = pl.BlockSpec(memory_space=pltpu.VMEM)
HBM = pl.BlockSpec(memory_space=pltpu.HBM)
DMA = pltpu.SemaphoreType.DMA
LIMIT = 56 * 2**20
WIDE = (2, 2, 4, 4)


def project(momentum, gradient, basis_rows):
    return pl.pallas_call(
        project_kernel,
        out_shape=[
            jax.ShapeDtypeStruct((ROWS, RANK), F32),
            jax.ShapeDtypeStruct((RANK, RANK), F32),
            jax.ShapeDtypeStruct((CUT, RANK), F32),
        ],
        in_specs=[HBM, HBM, HBM],
        out_specs=[VMEM, VMEM, VMEM],
        scratch_shapes=[
            pltpu.VMEM((NF * SLOT, PC), BF16),
            pltpu.VMEM((ROWS, COLS), BF16),
            pltpu.VMEM((ROWS, COLS), BF16),
            pltpu.VMEM((ROWS, COLS), BF16),
            pltpu.VMEM((OWN, COLS), BF16),
            pltpu.VMEM((NF * SLOT, RANK), BF16),
            pltpu.VMEM((ROWS, RANK), F32),
            pltpu.VMEM((8, 16, RANK), F32),
            pltpu.VMEM((RANK, RANK), F32),
            pltpu.VMEM((8, 8, 128), F32),
            pltpu.VMEM((8, 8, 128), F32),
            pltpu.VMEM((COLS, RANK), F32),
            pltpu.VMEM(WIDE + (CUT, RANK), F32),
            pltpu.VMEM((2, 4, CUT, RANK), F32),
            pltpu.VMEM((8, CUT, RANK), F32),
            DMA((3,)),
            DMA((8,)), DMA((8,)), DMA(WIDE), DMA(WIDE), DMA(WIDE), DMA(WIDE), DMA((2, 4)), DMA((8,)),
        ] + [DMA((8,))] * 12,
        compiler_params=pltpu.CompilerParams(collective_id=0, has_side_effects=True, vmem_limit_bytes=LIMIT),
        name="project",
    )(momentum, gradient, basis_rows)


def invert(gram):
    return pl.pallas_call(
        invert_kernel,
        out_shape=[jax.ShapeDtypeStruct((RANK, RANK), F32), jax.ShapeDtypeStruct((1,), F32)],
        in_specs=[VMEM],
        out_specs=[VMEM, pl.BlockSpec(memory_space=pltpu.SMEM)],
        scratch_shapes=[pltpu.VMEM((RANK, 2 * RANK), F32)],
        compiler_params=pltpu.CompilerParams(vmem_limit_bytes=LIMIT),
        name="invert",
    )(gram)


def back(momentum, gradient, proj, x, zown):
    return pl.pallas_call(
        back_kernel,
        out_shape=[
            jax.ShapeDtypeStruct((ROWS, COLS), BF16),
            jax.ShapeDtypeStruct((OWN, COLS), BF16),
            jax.ShapeDtypeStruct((ROWS, COLS), BF16),
        ],
        in_specs=[HBM, HBM, VMEM, VMEM, VMEM],
        out_specs=[VMEM, VMEM, VMEM],
        scratch_shapes=[
            pltpu.VMEM((ROWS, COLS), BF16),
            pltpu.VMEM((ROWS, COLS), BF16),
            pltpu.VMEM((ROWS, COLS), BF16),
            pltpu.VMEM((NF * PAD, RANK), BF16),
            pltpu.VMEM((ROWS, RANK), BF16),
            pltpu.VMEM((8, 8, RANK), F32),
            pltpu.VMEM((8, 8, RANK), F32),
            pltpu.VMEM((8, 8, RANK), F32),
            DMA((2,)),
            DMA((8,)), DMA((8,)), DMA(WIDE), DMA(WIDE),
        ] + [DMA((8,))] * 6,
        compiler_params=pltpu.CompilerParams(collective_id=1, has_side_effects=True, vmem_limit_bytes=LIMIT),
        name="back",
    )(momentum, gradient, proj, x, zown)


def direct(gram):
    lower_factor = jnp.linalg.cholesky(gram)
    return lax.linalg.triangular_solve(lower_factor, jnp.eye(RANK, dtype=F32), left_side=True, lower=True)


def local(momentum, gradient, basis_rows):
    proj, gram, zown = project(momentum, gradient, basis_rows)
    x, err = invert(gram)
    x = lax.cond(err[0] < 1e-5, lambda g, v: v, lambda g, v: direct(g), gram, x)
    return tuple(back(momentum, gradient, proj, x, zown))


def solution(mesh):
    return jax.shard_map(
        local,
        mesh=mesh,
        in_specs=(P("fsdp", "tp"), P("fsdp", "tp"), P("fsdp", "tp")),
        out_specs=(P("fsdp", "tp"), P("fsdp", "tp"), P("fsdp", "tp")),
        check_vma=False,
    )
```

```python
import functools
import math

import jax
import jax.numpy as jnp
from jax import lax
from jax.experimental import pallas as pl
from jax.experimental.pallas import tpu as pltpu
from jax.sharding import PartitionSpec as P

D = 8192
FF = 28672
RANK = 256
NY = 8
NZ = 8
NF = 64
NT = 8
ROWS = D // NF
COLS = FF // NT
OWN = RANK // NF
PARTS = 4
PC = COLS // PARTS
SLOT = 16
CUT = COLS // NF
PAD = 64

epsilon = 1e-06
momentum_decay = 0.95
UNIT = math.sqrt(D * FF / RANK)

F32 = jnp.float32
BF16 = jnp.bfloat16
MESH = pl.DeviceIdType.MESH
HIGHEST = lax.Precision.HIGHEST


def mod8(v):
    return lax.rem(v + 16, 8)


def place():
    f = lax.axis_index("fsdp")
    t = lax.axis_index("tp")
    y = f // NZ
    z = lax.rem(f, NZ)
    even = lax.rem(y + z, 2) == 0
    return f, t, y, z, even


def line(even, y, z, k):
    along_y = jnp.where(even, k, 0)
    along_z = jnp.where(even, 0, k)
    return mod8(y + along_y) * NZ + mod8(z + along_z)


def own_slot(even, y, z):
    return jnp.where(even, z * 4 + y // 2, 32 + y * 4 + z // 2)


def greet(f, t, y, z):
    barrier = pltpu.get_barrier_semaphore()
    for k in range(1, 8):
        pl.semaphore_signal(barrier, inc=1, device_id=(mod8(y + k) * NZ + z, t), device_id_type=MESH)
        pl.semaphore_signal(barrier, inc=1, device_id=(y * NZ + mod8(z + k), t), device_id_type=MESH)
        pl.semaphore_signal(barrier, inc=1, device_id=(f, mod8(t + k)), device_id_type=MESH)


def met():
    pl.semaphore_wait(pltpu.get_barrier_semaphore(), 21)


WAVE = (
    (0, None), (1, None), (3, None), (0, 0), (2, None), (1, 0), (3, 0), (0, 1), (2, 0), (1, 1), (3, 1), (0, 2),
    (2, 1), (1, 2), (3, 2), (0, 3), (2, 2), (1, 3), (3, 3), (2, 3),
)


def fourth(d, i):
    return (i < 2) if d == 0 else (i >= 2)


def slot_of(ax, origin, i):
    return ax * 32 + origin * 4 + i


def beside(ax, d, y, z):
    step = 1 if d == 0 else -1
    return (y * NZ + mod8(z + step)) if ax == 0 else (mod8(y + step) * NZ + z)


def gather(buf, size, f, t, y, z, even, s1, r1, s2, r2, between):
    rows = lambda slot: buf.at[pl.ds(pl.multiple_of(slot * size, size), size)]
    me = own_slot(even, y, z)
    at = (z, y)
    half = (y // 2, z // 2)
    home = (even, jnp.logical_not(even))
    here = jnp.where(even, y // 2, 4 + z // 2)
    aside = (f, mod8(t + 1))

    def straight(k, to):
        return pltpu.make_async_remote_copy(
            src_ref=rows(me), dst_ref=rows(me), send_sem=s1.at[k], recv_sem=r1.at[here],
            device_id=to, device_id_type=MESH,
        )

    def copy(ax, d, i, h, origin, to):
        slot = slot_of(ax, origin, i)
        return pltpu.make_async_remote_copy(
            src_ref=rows(slot), dst_ref=rows(slot), send_sem=s2.at[ax, d, i, h], recv_sem=r2.at[ax, d, i, h],
            device_id=to, device_id_type=MESH,
        )

    def send(ax, d, i, h):
        step = 1 if d == 0 else -1
        copy(ax, d, i, h, mod8(at[ax] - step * h), (beside(ax, d, y, z), t)).start()

    def landed(ax, d, i, h):
        step = 1 if d == 0 else -1
        copy(ax, d, i, h, mod8(at[ax] - step * (h + 1)), aside).wait_recv()

    for ax in range(2):
        @pl.when(home[ax])
        def _():
            for d in range(2):
                send(ax, d, half[ax], 0)
    for k in (1, 7, 2, 6, 3, 5, 4):
        straight(k, (line(even, y, z, k), t)).start()
    between[0]()
    for r, h in WAVE:
        for ax in range(2):
            i = lax.rem(half[ax] + r, 4)

            def first():
                slot = slot_of(ax, at[ax], i)
                pltpu.make_async_remote_copy(
                    src_ref=rows(slot), dst_ref=rows(slot), send_sem=s1.at[0], recv_sem=r1.at[ax * 4 + i],
                    device_id=aside, device_id_type=MESH,
                ).wait_recv()
                for d in range(2):
                    send(ax, d, i, 0)

            if h is None:
                if r == 0:
                    pl.when(jnp.logical_not(home[ax]))(first)
                else:
                    first()
                continue
            for d in range(2):
                if h < 2:
                    landed(ax, d, i, h)
                    send(ax, d, i, h + 1)
                elif h == 2:
                    landed(ax, d, i, h)

                    @pl.when(fourth(d, i))
                    def _():
                        send(ax, d, i, 3)
                else:

                    @pl.when(fourth(d, i))
                    def _():
                        landed(ax, d, i, 3)
        if r == 2:
            between[1 if h is None else h + 2]()

    def finish():
        for k in range(1, 8):
            straight(k, aside).wait_send()
        for ax in range(2):
            for d in range(2):
                for i in range(4):
                    for h in range(4 if fourth(d, i) else 3):
                        copy(ax, d, i, h, at[ax], aside).wait_send()

    return finish


def exchange(src_of, dst_of, ids, pos, send, recv):
    copies = []
    for k in (4, 3, 5, 2, 6, 1, 7):
        p = mod8(pos + k)
        copy = pltpu.make_async_remote_copy(
            src_ref=src_of(p),
            dst_ref=dst_of(pos),
            send_sem=send.at[k],
            recv_sem=recv.at[8 - k],
            device_id=ids(p),
            device_id_type=MESH,
        )
        copy.start()
        copies.append(copy)
    return copies


def arrived(dst_of, ids, pos, send, recv):
    for k in range(1, 8):
        p = mod8(pos + k)
        pltpu.make_async_remote_copy(
            src_ref=dst_of(p),
            dst_ref=dst_of(p),
            send_sem=send.at[k],
            recv_sem=recv.at[k],
            device_id=ids(p),
            device_id_type=MESH,
        ).wait_recv()


def start_inverse(gram, sx):
    i = lax.broadcasted_iota(jnp.int32, (RANK, RANK), 0)
    j = lax.broadcasted_iota(jnp.int32, (RANK, RANK), 1)
    on = jnp.where(i == j, gram, 0.0)
    down = lax.rsqrt(jnp.sum(on, axis=1, keepdims=True))
    across = lax.rsqrt(jnp.sum(on, axis=0, keepdims=True))
    sx[:, :RANK] = gram * down * across
    sx[:, RANK:] = jnp.where(i == j, down, 0.0)


def step_inverse(sx):
    i = lax.broadcasted_iota(jnp.int32, (RANK, RANK), 0)
    j = lax.broadcasted_iota(jnp.int32, (RANK, RANK), 1)
    e = sx[:, :RANK] - jnp.where(i == j, 1.0, 0.0)
    w = jnp.where(i > j, -e, jnp.where(i == j, 1.0 - 0.5 * e, 0.0))
    out = jnp.dot(w, sx[...], precision=HIGHEST, preferred_element_type=F32)
    sx[:, RANK:] = out[:, RANK:]
    sx[:, :RANK] = lax.dot_general(
        out[:, :RANK], w, (((1,), (1,)), ((), ())), precision=HIGHEST, preferred_element_type=F32
    )


def missed(sx):
    i = lax.broadcasted_iota(jnp.int32, (RANK, RANK), 0)
    j = lax.broadcasted_iota(jnp.int32, (RANK, RANK), 1)
    e = sx[:, :RANK] - jnp.where(i == j, 1.0, 0.0)
    return jnp.sum(e * e, axis=0, keepdims=True)


def spread(zown, x, proj, low_ref, back_ref, sq_ref, place_, q1, q2, q3, sems, ready):
    f, t, y, z, even = place_
    s1, r1, s2, r2, e1, f1, e2, f2, e3, f3 = sems
    me = own_slot(even, y, z)
    tp_id = lambda p: (f, p)
    y_id = lambda p: (p * NZ + z, t)
    z_id = lambda p: (y * NZ + p, t)
    turn = (((1,), (1,)), ((), ()))
    mine = lax.dot_general(zown, x(), turn, precision=HIGHEST, preferred_element_type=F32)
    back_ref[pl.ds(pl.multiple_of(me * PAD, PAD), PAD), :] = jnp.concatenate(
        [mine, jnp.zeros((PAD - CUT, RANK), F32)], axis=0
    ).astype(BF16)
    q1[t] = jnp.broadcast_to(jnp.sum(mine * mine, axis=0, keepdims=True), (8, RANK))
    ready()
    waits = []

    def open_squares():
        waits.extend(exchange(lambda p: q1.at[t], lambda p: q1.at[p], tp_id, t, e1, f1))
        low_ref[...] = lax.dot_general(
            proj(), x(), turn, precision=HIGHEST, preferred_element_type=F32
        ).astype(BF16)

    def fold(buf):
        sums = buf[0]
        for p in range(1, 8):
            sums = sums + buf[p]
        return sums

    def over_y():
        arrived(lambda p: q1.at[p], tp_id, t, e1, f1)
        q2[y] = fold(q1)
        waits.extend(exchange(lambda p: q2.at[y], lambda p: q2.at[p], y_id, y, e2, f2))

    def over_z():
        arrived(lambda p: q2.at[p], y_id, y, e2, f2)
        q3[z] = fold(q2)
        waits.extend(exchange(lambda p: q3.at[z], lambda p: q3.at[p], z_id, z, e3, f3))

    nothing = lambda: None
    finish = gather(
        back_ref, PAD, f, t, y, z, even, s1, r1, s2, r2,
        [open_squares, over_y, over_z, nothing, nothing, nothing],
    )
    arrived(lambda p: q3.at[p], z_id, z, e3, f3)
    sq_ref[...] = fold(q3)
    finish()
    for copy in waits:
        copy.wait_send()


def thirds(v):
    a1 = v.astype(BF16)
    rest = v - a1.astype(F32)
    a2 = rest.astype(BF16)
    return a1, a2, (rest - a2.astype(F32)).astype(BF16)


def project_kernel(
    m_ref, g_ref, basis_ref, proj_ref, gram_ref, z_ref, err_ref, low_ref, back_ref, sq_ref,
    vbuf, bbuf, mbuf, gbuf, stage, sel, part, tbuf, gpart, ybuf, zbuf, work, land, near, far, sx, q1, q2, q3,
    local_sem, s1, r1, s2, r2, s3, r3, s4, r4, s5, r5, s6, r6, ps, pr, as_, ar, ys, yr, zs, zr, bs, br, ts, tr,
    e1, f1, e2, f2, e3, f3,
):
    f, t, y, z, even = place()
    me = own_slot(even, y, z)
    at = (z, y)
    aside = (f, mod8(t + 1))
    cm = pltpu.make_async_copy(m_ref, mbuf, local_sem.at[0])
    cg = pltpu.make_async_copy(g_ref, gbuf, local_sem.at[1])
    cb = pltpu.make_async_copy(basis_ref, stage, local_sem.at[2])
    cb.start()
    cm.start()
    cg.start()
    greet(f, t, y, z)
    cb.wait()
    own = stage[...].astype(F32)
    pieces = [own[:, j * PC:(j + 1) * PC] for j in range(PARTS)]
    vbuf[pl.ds(pl.multiple_of(me * SLOT, SLOT), SLOT), :] = jnp.concatenate(pieces, axis=0).astype(BF16)
    met()

    def prepare():
        cm.wait()
        cg.wait()
        for j in range(PARTS):
            cols = slice(j * PC, (j + 1) * PC)
            bbuf[:, cols] = (mbuf[:, cols].astype(F32) + gbuf[:, cols].astype(F32)).astype(BF16)
        part[...] = jnp.zeros((ROWS, RANK), F32)

        def choose(i, carry):
            base = pl.multiple_of(i * 128, 128)
            row = base + lax.broadcasted_iota(jnp.int32, (128, RANK), 0)
            slot = row // SLOT
            first, second = (slot // 4) % 8, slot % 4
            yf = 2 * second + (first % 2)
            zo = 2 * second + (1 - first % 2)
            dev = jnp.where(slot < 32, yf * NZ + first, first * NZ + zo)
            hit = dev * OWN + row % 4 == lax.broadcasted_iota(jnp.int32, (128, RANK), 1)
            sel[pl.ds(base, 128), :] = jnp.where(hit, 1.0, 0.0).astype(BF16)
            return carry

        lax.fori_loop(0, 8, choose, 0)

    def level(h):
        def run():
            if h == 0 or h == 4:
                starts = [slot_of(ax, mod8(at[ax] + h), 0) * SLOT for ax in range(2)]
            else:
                starts = [slot_of(ax, mod8(at[ax] + s), 0) * SLOT for ax in range(2) for s in (h, -h)]
            spans = [pl.ds(pl.multiple_of(s, 64), 64) for s in starts]
            v = jnp.concatenate([vbuf[s, :] for s in spans], axis=0)
            pick = jnp.concatenate([sel[s, :] for s in spans], axis=0)
            piece_of = (lax.broadcasted_iota(jnp.int32, (ROWS, v.shape[0]), 1) // 4) % 4
            acc = jnp.zeros((ROWS, v.shape[0]), F32)
            for j in range(PARTS):
                got = lax.dot_general(
                    bbuf[:, j * PC:(j + 1) * PC], v, (((1,), (1,)), ((), ())), preferred_element_type=F32
                )
                acc = jnp.where(piece_of == j, got, acc)
            total = part[...]
            for a in thirds(acc)[::-1]:
                total = total + jnp.dot(a, pick, preferred_element_type=F32)
            part[...] = total
        return run

    finish = gather(
        vbuf, SLOT, f, t, y, z, even, s1, r1, s2, r2,
        [prepare, level(0), level(1), level(2), level(3), level(4)],
    )

    tp_id = lambda p: (f, p)
    y_id = lambda p: (p * NZ + z, t)
    z_id = lambda p: (y * NZ + p, t)

    slab = lambda p: pl.ds(pl.multiple_of(p * 16, 16), 16)
    c1 = exchange(lambda p: part.at[slab(p)], lambda p: tbuf.at[p], tp_id, t, ps, pr)
    tbuf[t] = part[slab(t), :]
    arrived(lambda p: tbuf.at[p], tp_id, t, ps, pr)
    sums = tbuf[0]
    for p in range(1, 8):
        sums = sums + tbuf[p]
    proj_ref[slab(t), :] = sums
    c2 = exchange(lambda p: proj_ref.at[slab(t)], lambda p: proj_ref.at[slab(p)], tp_id, t, as_, ar)
    arrived(lambda p: proj_ref.at[slab(p)], tp_id, t, as_, ar)

    pv = proj_ref[...]
    gpart[...] = lax.dot_general(pv, pv, (((0,), (0,)), ((), ())), precision=HIGHEST, preferred_element_type=F32)
    tile = lambda p: (
        pl.ds(pl.multiple_of(t * 32 + (p // 2) * 8, 8), 8),
        pl.ds(pl.multiple_of(lax.rem(p, 2) * 128, 128), 128),
    )
    c3 = exchange(lambda p: gpart.at[tile(p)], lambda p: ybuf.at[p], y_id, y, ys, yr)
    ybuf[y] = gpart[tile(y)]

    split = thirds(pv)
    for j in range(7):
        cols = slice(j * 512, (j + 1) * 512)
        total = jnp.zeros((512, RANK), F32)
        for a in split[::-1]:
            total = total + lax.dot_general(
                bbuf[:, cols], a, (((0,), (0,)), ((), ())), preferred_element_type=F32
            )
        work[cols, :] = total
    cut = lambda ax, origin, i: pl.ds(pl.multiple_of(slot_of(ax, origin, i) * CUT, 8), CUT)
    streams = [(ax, d, i) for i in range(4) for ax in range(2) for d in range(2)]
    hops = lambda d, i: 4 if fourth(d, i) else 3
    sent = []

    def pass_on(ax, d, i, h, src):
        copy = pltpu.make_async_remote_copy(
            src_ref=src, dst_ref=land.at[ax, d, i, h], send_sem=s3.at[ax, d, i, h], recv_sem=r3.at[ax, d, i, h],
            device_id=(beside(ax, d, y, z), t), device_id_type=MESH,
        )
        copy.start()
        sent.append(copy)

    def came(ax, d, i, h):
        pltpu.make_async_remote_copy(
            src_ref=land.at[ax, d, i, h], dst_ref=land.at[ax, d, i, h], send_sem=s3.at[ax, d, i, h],
            recv_sem=r3.at[ax, d, i, h], device_id=aside, device_id_type=MESH,
        ).wait_recv()

    def ring(h):
        for ax, d, i in streams:
            n = hops(d, i)
            if h < n:
                came(ax, d, i, h)
                if h + 1 < n:
                    step = 1 if d == 0 else -1
                    land[ax, d, i, h] = land[ax, d, i, h] + work[cut(ax, mod8(at[ax] + step * (n - h - 1)), i), :]
                    pass_on(ax, d, i, h + 1, land.at[ax, d, i, h])

    for ax, d, i in streams:
        step = 1 if d == 0 else -1
        pass_on(ax, d, i, 0, work.at[cut(ax, mod8(at[ax] + step * hops(d, i)), i)])
    arrived(lambda p: ybuf.at[p], y_id, y, ys, yr)
    sums = ybuf[0]
    for p in range(1, 8):
        sums = sums + ybuf[p]
    zbuf[z] = sums
    c4 = exchange(lambda p: zbuf.at[z], lambda p: zbuf.at[p], z_id, z, zs, zr)
    ring(0)
    arrived(lambda p: zbuf.at[p], z_id, z, zs, zr)
    sums = zbuf[0]
    for p in range(1, 8):
        sums = sums + zbuf[p]
    gram_ref[tile(y)] = sums
    c5 = exchange(lambda p: gram_ref.at[tile(y)], lambda p: gram_ref.at[tile(p)], y_id, y, bs, br)
    ring(1)
    arrived(lambda p: gram_ref.at[tile(p)], y_id, y, bs, br)
    block = lambda p: pl.ds(pl.multiple_of(p * 32, 32), 32)
    c6 = exchange(lambda p: gram_ref.at[block(t)], lambda p: gram_ref.at[block(p)], tp_id, t, ts, tr)
    ring(2)
    ring(3)

    spot = jnp.where(even, y, z)

    def target(ax, i):
        odd = lax.rem(at[ax], 2) if ax == 0 else 1 - lax.rem(at[ax], 2)
        return 2 * i + odd

    def cross(ax, i, device):
        return pltpu.make_async_remote_copy(
            src_ref=near.at[ax, i], dst_ref=far.at[at[1 - ax]], send_sem=s4.at[ax, i], recv_sem=r4.at[at[1 - ax]],
            device_id=device, device_id_type=MESH,
        )

    for ax in range(2):
        for i in range(4):
            both = work[cut(ax, at[ax], i), :]
            for d in range(2):
                both = both + land[ax, d, i, hops(d, i) - 1]
            near[ax, i] = both
            to = target(ax, i)

            @pl.when(to != at[1 - ax])
            def _():
                cross(ax, i, ((to * NZ + z) if ax == 0 else (y * NZ + to), t)).start()

            @pl.when(to == at[1 - ax])
            def _():
                far[at[1 - ax]] = both

    arrived(lambda p: gram_ref.at[block(p)], tp_id, t, ts, tr)
    start_inverse(gram_ref[...], sx)

    def advance(i, carry):
        step_inverse(sx)
        return carry

    lax.fori_loop(0, 6, advance, 0)
    err_ref[...] = missed(sx)
    for k in range(1, 8):
        p = mod8(spot + k)
        pltpu.make_async_remote_copy(
            src_ref=far.at[p], dst_ref=far.at[p], send_sem=s4.at[0, 0], recv_sem=r4.at[p],
            device_id=aside, device_id_type=MESH,
        ).wait_recv()
    sums = far[0]
    for p in range(1, 8):
        sums = sums + far[p]
    z_ref[...] = sums
    sems = (s5, r5, s6, r6, e1, f1, e2, f2, e3, f3)
    spread(
        sums, lambda: sx[:, RANK:], lambda: proj_ref[...], low_ref, back_ref, sq_ref, (f, t, y, z, even), q1, q2, q3, sems,
        lambda: None,
    )
    finish()
    for copies in (c1, c2, c3, c4, c5, c6, sent):
        for copy in copies:
            copy.wait_send()
    for ax in range(2):
        for i in range(4):
            @pl.when(target(ax, i) != at[1 - ax])
            def _():
                cross(ax, i, aside).wait_send()


def again_kernel(
    proj_ref, x_ref, z_ref, low_ref, back_ref, sq_ref, q1, q2, q3, s1, r1, s2, r2, e1, f1, e2, f2, e3, f3
):
    where = place()
    greet(*where[:4])
    sems = (s1, r1, s2, r2, e1, f1, e2, f2, e3, f3)
    spread(
        z_ref[...], lambda: x_ref[...], lambda: proj_ref[...], low_ref, back_ref, sq_ref, where, q1, q2, q3, sems, met
    )


def output_kernel(m_ref, g_ref, low_ref, back_ref, sq_ref, mom_ref, own_ref, upd_ref):
    f = lax.axis_index("fsdp")
    squares = sq_ref[0:1, :] + epsilon
    low = low_ref[...]
    scaled = (low.astype(F32) * jnp.sqrt(squares).astype(BF16).astype(F32)).astype(BF16)
    pick = jnp.where(
        lax.broadcasted_iota(jnp.int32, (8, RANK), 0) + f * OWN == lax.broadcasted_iota(jnp.int32, (8, RANK), 1),
        1.0, 0.0,
    ).astype(BF16)
    turn = (((1,), (1,)), ((), ()))
    pieces = [back_ref[s * PAD:s * PAD + CUT, :].astype(F32) for s in range(16)]
    nb = (jnp.concatenate(pieces, axis=0) * lax.rsqrt(squares)).astype(BF16)
    buffer = (m_ref[...].astype(F32) + g_ref[...].astype(F32)).astype(BF16).astype(F32)
    own_ref[...] = lax.dot_general(pick, nb, turn, preferred_element_type=F32)[0:OWN].astype(BF16)
    upd_ref[...] = (UNIT * lax.dot_general(low, nb, turn, preferred_element_type=F32)).astype(BF16)
    mom_ref[...] = (
        buffer - (1.0 - momentum_decay) * lax.dot_general(scaled, nb, turn, preferred_element_type=F32)
    ).astype(BF16)


VMEM = pl.BlockSpec(memory_space=pltpu.VMEM)
HBM = pl.BlockSpec(memory_space=pltpu.HBM)
DMA = pltpu.SemaphoreType.DMA
LIMIT = 56 * 2**20
WIDE = (2, 2, 4, 4)
SPREAD = [
    jax.ShapeDtypeStruct((ROWS, RANK), BF16),
    jax.ShapeDtypeStruct((NF * PAD, RANK), BF16),
    jax.ShapeDtypeStruct((8, RANK), F32),
]


def project(momentum, gradient, basis_rows):
    return pl.pallas_call(
        project_kernel,
        out_shape=[
            jax.ShapeDtypeStruct((ROWS, RANK), F32),
            jax.ShapeDtypeStruct((RANK, RANK), F32),
            jax.ShapeDtypeStruct((CUT, RANK), F32),
            jax.ShapeDtypeStruct((1, RANK), F32),
        ] + SPREAD,
        in_specs=[HBM, HBM, HBM],
        out_specs=[VMEM] * 7,
        scratch_shapes=[
            pltpu.VMEM((NF * SLOT, PC), BF16),
            pltpu.VMEM((ROWS, COLS), BF16),
            pltpu.VMEM((ROWS, COLS), BF16),
            pltpu.VMEM((ROWS, COLS), BF16),
            pltpu.VMEM((OWN, COLS), BF16),
            pltpu.VMEM((NF * SLOT, RANK), BF16),
            pltpu.VMEM((ROWS, RANK), F32),
            pltpu.VMEM((8, 16, RANK), F32),
            pltpu.VMEM((RANK, RANK), F32),
            pltpu.VMEM((8, 8, 128), F32),
            pltpu.VMEM((8, 8, 128), F32),
            pltpu.VMEM((COLS, RANK), F32),
            pltpu.VMEM(WIDE + (CUT, RANK), F32),
            pltpu.VMEM((2, 4, CUT, RANK), F32),
            pltpu.VMEM((8, CUT, RANK), F32),
            pltpu.VMEM((RANK, 2 * RANK), F32),
            pltpu.VMEM((8, 8, RANK), F32),
            pltpu.VMEM((8, 8, RANK), F32),
            pltpu.VMEM((8, 8, RANK), F32),
            DMA((3,)),
            DMA((8,)), DMA((8,)), DMA(WIDE), DMA(WIDE), DMA(WIDE), DMA(WIDE), DMA((2, 4)), DMA((8,)),
            DMA((8,)), DMA((8,)), DMA(WIDE), DMA(WIDE),
        ] + [DMA((8,))] * 18,
        compiler_params=pltpu.CompilerParams(collective_id=0, has_side_effects=True, vmem_limit_bytes=LIMIT),
        name="project",
    )(momentum, gradient, basis_rows)


def again(proj, x, zown):
    return pl.pallas_call(
        again_kernel,
        out_shape=SPREAD,
        in_specs=[VMEM] * 3,
        out_specs=[VMEM] * 3,
        scratch_shapes=[pltpu.VMEM((8, 8, RANK), F32)] * 3
        + [DMA((8,)), DMA((8,)), DMA(WIDE), DMA(WIDE)]
        + [DMA((8,))] * 6,
        compiler_params=pltpu.CompilerParams(collective_id=1, has_side_effects=True, vmem_limit_bytes=LIMIT),
        name="again",
    )(proj, x, zown)


def outputs(momentum, gradient, low, back, squares):
    tall = pl.BlockSpec((ROWS, PC), lambda j: (0, j))
    return pl.pallas_call(
        output_kernel,
        out_shape=[
            jax.ShapeDtypeStruct((ROWS, COLS), BF16),
            jax.ShapeDtypeStruct((OWN, COLS), BF16),
            jax.ShapeDtypeStruct((ROWS, COLS), BF16),
        ],
        grid=(PARTS,),
        in_specs=[
            tall,
            tall,
            pl.BlockSpec((ROWS, RANK), lambda j: (0, 0)),
            pl.BlockSpec((16 * PAD, RANK), lambda j: (j, 0)),
            pl.BlockSpec((8, RANK), lambda j: (0, 0)),
        ],
        out_specs=[tall, pl.BlockSpec((OWN, PC), lambda j: (0, j)), tall],
        compiler_params=pltpu.CompilerParams(vmem_limit_bytes=LIMIT),
        name="outputs",
    )(momentum, gradient, low, back, squares)


def direct(gram):
    lower_factor = jnp.linalg.cholesky(gram)
    return lax.linalg.triangular_solve(lower_factor, jnp.eye(RANK, dtype=F32), left_side=True, lower=True)


def local(momentum, gradient, basis_rows):
    proj, gram, zown, err, low, back, squares = project(momentum, gradient, basis_rows)
    low, back, squares = lax.cond(
        jnp.sum(err) < 1e-8,
        lambda proj, gram, zown, *now: now,
        lambda proj, gram, zown, *now: tuple(again(proj, direct(gram), zown)),
        proj, gram, zown, low, back, squares,
    )
    return tuple(outputs(momentum, gradient, low, back, squares))


def solution(mesh):
    return jax.shard_map(
        local,
        mesh=mesh,
        in_specs=(P("fsdp", "tp"), P("fsdp", "tp"), P("fsdp", "tp")),
        out_specs=(P("fsdp", "tp"), P("fsdp", "tp"), P("fsdp", "tp")),
        check_vma=False,
    )
```

```python
import functools
import math

import jax
import jax.numpy as jnp
from jax import lax
from jax.experimental import pallas as pl
from jax.experimental.pallas import tpu as pltpu
from jax.sharding import PartitionSpec as P

D = 8192
FF = 28672
RANK = 256
NY = 8
NZ = 8
NF = 64
NT = 8
ROWS = D // NF
COLS = FF // NT
OWN = RANK // NF
PARTS = 4
PC = COLS // PARTS
SLOT = 16
CUT = COLS // NF
PACK = 2 * CUT
HALF = RANK // 2

epsilon = 1e-06
momentum_decay = 0.95
UNIT = math.sqrt(D * FF / RANK)

F32 = jnp.float32
BF16 = jnp.bfloat16
MESH = pl.DeviceIdType.MESH
HIGHEST = lax.Precision.HIGHEST


def mod8(v):
    return lax.rem(v + 16, 8)


def place():
    f = lax.axis_index("fsdp")
    t = lax.axis_index("tp")
    y = f // NZ
    z = lax.rem(f, NZ)
    even = lax.rem(y + z, 2) == 0
    return f, t, y, z, even


def line(even, y, z, k):
    along_y = jnp.where(even, k, 0)
    along_z = jnp.where(even, 0, k)
    return mod8(y + along_y) * NZ + mod8(z + along_z)


def own_slot(even, y, z):
    return jnp.where(even, z * 4 + y // 2, 32 + y * 4 + z // 2)


def greet(f, t, y, z):
    barrier = pltpu.get_barrier_semaphore()
    for k in range(1, 8):
        pl.semaphore_signal(barrier, inc=1, device_id=(mod8(y + k) * NZ + z, t), device_id_type=MESH)
        pl.semaphore_signal(barrier, inc=1, device_id=(y * NZ + mod8(z + k), t), device_id_type=MESH)
        pl.semaphore_signal(barrier, inc=1, device_id=(f, mod8(t + k)), device_id_type=MESH)


def met():
    pl.semaphore_wait(pltpu.get_barrier_semaphore(), 21)


WAVE = (
    (0, None), (1, None), (3, None), (0, 0), (2, None), (1, 0), (3, 0), (0, 1), (2, 0), (1, 1), (3, 1), (0, 2),
    (2, 1), (1, 2), (3, 2), (0, 3), (2, 2), (1, 3), (3, 3), (2, 3),
)


def fourth(d, i):
    return (i < 2) if d == 0 else (i >= 2)


def slot_of(ax, origin, i):
    return ax * 32 + origin * 4 + i


def beside(ax, d, y, z):
    step = 1 if d == 0 else -1
    return (y * NZ + mod8(z + step)) if ax == 0 else (mod8(y + step) * NZ + z)


def gather(buf, size, f, t, y, z, even, s1, r1, s2, r2, between):
    rows = lambda slot: buf.at[pl.ds(pl.multiple_of(slot * size, size), size)]
    me = own_slot(even, y, z)
    at = (z, y)
    half = (y // 2, z // 2)
    home = (even, jnp.logical_not(even))
    here = jnp.where(even, y // 2, 4 + z // 2)
    aside = (f, mod8(t + 1))

    def straight(k, to):
        return pltpu.make_async_remote_copy(
            src_ref=rows(me), dst_ref=rows(me), send_sem=s1.at[k], recv_sem=r1.at[here],
            device_id=to, device_id_type=MESH,
        )

    def copy(ax, d, i, h, origin, to):
        slot = slot_of(ax, origin, i)
        return pltpu.make_async_remote_copy(
            src_ref=rows(slot), dst_ref=rows(slot), send_sem=s2.at[ax, d, i, h], recv_sem=r2.at[ax, d, i, h],
            device_id=to, device_id_type=MESH,
        )

    def send(ax, d, i, h):
        step = 1 if d == 0 else -1
        copy(ax, d, i, h, mod8(at[ax] - step * h), (beside(ax, d, y, z), t)).start()

    def landed(ax, d, i, h):
        step = 1 if d == 0 else -1
        copy(ax, d, i, h, mod8(at[ax] - step * (h + 1)), aside).wait_recv()

    for ax in range(2):
        @pl.when(home[ax])
        def _():
            for d in range(2):
                send(ax, d, half[ax], 0)
    for k in (1, 7, 2, 6, 3, 5, 4):
        straight(k, (line(even, y, z, k), t)).start()
    between[0]()
    for r, h in WAVE:
        for ax in range(2):
            i = lax.rem(half[ax] + r, 4)

            def first():
                slot = slot_of(ax, at[ax], i)
                pltpu.make_async_remote_copy(
                    src_ref=rows(slot), dst_ref=rows(slot), send_sem=s1.at[0], recv_sem=r1.at[ax * 4 + i],
                    device_id=aside, device_id_type=MESH,
                ).wait_recv()
                for d in range(2):
                    send(ax, d, i, 0)

            if h is None:
                if r == 0:
                    pl.when(jnp.logical_not(home[ax]))(first)
                else:
                    first()
                continue
            for d in range(2):
                if h < 2:
                    landed(ax, d, i, h)
                    send(ax, d, i, h + 1)
                elif h == 2:
                    landed(ax, d, i, h)

                    @pl.when(fourth(d, i))
                    def _():
                        send(ax, d, i, 3)
                else:

                    @pl.when(fourth(d, i))
                    def _():
                        landed(ax, d, i, 3)
        if r == 2:
            between[1 if h is None else h + 2]()

    def finish():
        for k in range(1, 8):
            straight(k, aside).wait_send()
        for ax in range(2):
            for d in range(2):
                for i in range(4):
                    for h in range(4 if fourth(d, i) else 3):
                        copy(ax, d, i, h, at[ax], aside).wait_send()

    return finish


def exchange(src_of, dst_of, ids, pos, send, recv):
    copies = []
    for k in (4, 3, 5, 2, 6, 1, 7):
        p = mod8(pos + k)
        copy = pltpu.make_async_remote_copy(
            src_ref=src_of(p),
            dst_ref=dst_of(pos),
            send_sem=send.at[k],
            recv_sem=recv.at[8 - k],
            device_id=ids(p),
            device_id_type=MESH,
        )
        copy.start()
        copies.append(copy)
    return copies


def arrived(dst_of, ids, pos, send, recv):
    for k in range(1, 8):
        p = mod8(pos + k)
        pltpu.make_async_remote_copy(
            src_ref=dst_of(p),
            dst_ref=dst_of(p),
            send_sem=send.at[k],
            recv_sem=recv.at[k],
            device_id=ids(p),
            device_id_type=MESH,
        ).wait_recv()


def start_inverse(gram, sx):
    i = lax.broadcasted_iota(jnp.int32, (RANK, RANK), 0)
    j = lax.broadcasted_iota(jnp.int32, (RANK, RANK), 1)
    on = jnp.where(i == j, gram, 0.0)
    down = lax.rsqrt(jnp.sum(on, axis=1, keepdims=True))
    across = lax.rsqrt(jnp.sum(on, axis=0, keepdims=True))
    sx[:, :RANK] = gram * down * across
    sx[:, RANK:] = jnp.where(i == j, down, 0.0)


def step_inverse(sx):
    i = lax.broadcasted_iota(jnp.int32, (RANK, RANK), 0)
    j = lax.broadcasted_iota(jnp.int32, (RANK, RANK), 1)
    e = sx[:, :RANK] - jnp.where(i == j, 1.0, 0.0)
    w = jnp.where(i > j, -e, jnp.where(i == j, 1.0 - 0.5 * e, 0.0))
    out = jnp.dot(w, sx[...], precision=HIGHEST, preferred_element_type=F32)
    sx[:, RANK:] = out[:, RANK:]
    sx[:, :RANK] = lax.dot_general(
        out[:, :RANK], w, (((1,), (1,)), ((), ())), precision=HIGHEST, preferred_element_type=F32
    )


def missed(sx):
    i = lax.broadcasted_iota(jnp.int32, (RANK, RANK), 0)
    j = lax.broadcasted_iota(jnp.int32, (RANK, RANK), 1)
    e = sx[:, :RANK] - jnp.where(i == j, 1.0, 0.0)
    return jnp.sum(e * e)


def pack(columns):
    return jnp.concatenate([columns[:, :HALF], columns[:, HALF:]], axis=0).astype(BF16)


def spread(zown, sx, proj_ref, check_ref, low_ref, back_ref, sq_ref, where, q1, q2, q3, sems):
    f, t, y, z, even = where
    s1, r1, s2, r2, e1, f1, e2, f2, e3, f3 = sems
    me = own_slot(even, y, z)
    tp_id = lambda p: (f, p)
    y_id = lambda p: (p * NZ + z, t)
    z_id = lambda p: (y * NZ + p, t)
    turn = (((1,), (1,)), ((), ()))
    mine = lax.dot_general(zown, sx[:, RANK:], turn, precision=HIGHEST, preferred_element_type=F32)
    back_ref[pl.ds(pl.multiple_of(me * PACK, 16), PACK), :] = pack(mine)
    first = lax.broadcasted_iota(jnp.int32, (8, RANK), 0) == 0
    q1[t] = jnp.where(
        first, jnp.sum(mine * mine, axis=0, keepdims=True), jnp.sum(zown * zown, axis=0, keepdims=True)
    )
    waits = []

    def open_squares():
        waits.extend(exchange(lambda p: q1.at[t], lambda p: q1.at[p], tp_id, t, e1, f1))
        low_ref[...] = lax.dot_general(
            proj_ref[...], sx[:, RANK:], turn, precision=HIGHEST, preferred_element_type=F32
        ).astype(BF16)

    def fold(buf):
        sums = buf[0]
        for p in range(1, 8):
            sums = sums + buf[p]
        return sums

    def over_y():
        arrived(lambda p: q1.at[p], tp_id, t, e1, f1)
        q2[y] = fold(q1)
        waits.extend(exchange(lambda p: q2.at[y], lambda p: q2.at[p], y_id, y, e2, f2))

    def over_z():
        arrived(lambda p: q2.at[p], y_id, y, e2, f2)
        q3[z] = fold(q2)
        waits.extend(exchange(lambda p: q3.at[z], lambda p: q3.at[p], z_id, z, e3, f3))

    nothing = lambda: None
    finish = gather(
        back_ref, PACK, f, t, y, z, even, s1, r1, s2, r2,
        [open_squares, over_y, over_z, nothing, nothing, nothing],
    )
    arrived(lambda p: q3.at[p], z_id, z, e3, f3)
    squares = fold(q3)
    sq_ref[...] = squares
    x = sx[:, RANK:]
    grown = lax.dot_general(squares, x * x, turn, precision=HIGHEST, preferred_element_type=F32)[1:2, :]
    check_ref[1] = jnp.sum(grown / squares[0:1, :]) * (1.0 / RANK)
    finish()
    for copy in waits:
        copy.wait_send()


def thirds(v):
    a1 = v.astype(BF16)
    rest = v - a1.astype(F32)
    a2 = rest.astype(BF16)
    return a1, a2, (rest - a2.astype(F32)).astype(BF16)


def project_kernel(
    m_ref, g_ref, basis_ref, proj_ref, gram_ref, check_ref, b_ref, low_ref, back_ref, sq_ref,
    vbuf, mbuf, gbuf, stage, sel, part, tbuf, gpart, ybuf, zbuf, work, land, near, far, sx, q1, q2, q3,
    local_sem, s1, r1, s2, r2, s3, r3, s4, r4, s5, r5, s6, r6, ps, pr, as_, ar, ys, yr, zs, zr, bs, br, ts, tr,
    e1, f1, e2, f2, e3, f3,
):
    f, t, y, z, even = place()
    me = own_slot(even, y, z)
    at = (z, y)
    aside = (f, mod8(t + 1))
    cm = pltpu.make_async_copy(m_ref, mbuf, local_sem.at[0])
    cg = pltpu.make_async_copy(g_ref, gbuf, local_sem.at[1])
    cb = pltpu.make_async_copy(basis_ref, stage, local_sem.at[2])
    cb.start()
    cm.start()
    cg.start()
    greet(f, t, y, z)
    cb.wait()
    own = stage[...].astype(F32)
    pieces = [own[:, j * PC:(j + 1) * PC] for j in range(PARTS)]
    vbuf[pl.ds(pl.multiple_of(me * SLOT, SLOT), SLOT), :] = jnp.concatenate(pieces, axis=0).astype(BF16)
    met()

    def prepare():
        cm.wait()
        cg.wait()
        for j in range(PARTS):
            cols = slice(j * PC, (j + 1) * PC)
            b_ref[:, cols] = (mbuf[:, cols].astype(F32) + gbuf[:, cols].astype(F32)).astype(BF16)
        part[...] = jnp.zeros((ROWS, RANK), F32)

        def choose(i, carry):
            base = pl.multiple_of(i * 128, 128)
            row = base + lax.broadcasted_iota(jnp.int32, (128, RANK), 0)
            slot = row // SLOT
            first, second = (slot // 4) % 8, slot % 4
            yf = 2 * second + (first % 2)
            zo = 2 * second + (1 - first % 2)
            dev = jnp.where(slot < 32, yf * NZ + first, first * NZ + zo)
            hit = dev * OWN + row % 4 == lax.broadcasted_iota(jnp.int32, (128, RANK), 1)
            sel[pl.ds(base, 128), :] = jnp.where(hit, 1.0, 0.0).astype(BF16)
            return carry

        lax.fori_loop(0, 8, choose, 0)

    def level(h):
        def run():
            if h == 0 or h == 4:
                starts = [slot_of(ax, mod8(at[ax] + h), 0) * SLOT for ax in range(2)]
            else:
                starts = [slot_of(ax, mod8(at[ax] + s), 0) * SLOT for ax in range(2) for s in (h, -h)]
            spans = [pl.ds(pl.multiple_of(s, 64), 64) for s in starts]
            v = jnp.concatenate([vbuf[s, :] for s in spans], axis=0)
            pick = jnp.concatenate([sel[s, :] for s in spans], axis=0)
            piece_of = (lax.broadcasted_iota(jnp.int32, (ROWS, v.shape[0]), 1) // 4) % 4
            acc = jnp.zeros((ROWS, v.shape[0]), F32)
            for j in range(PARTS):
                got = lax.dot_general(
                    b_ref[:, j * PC:(j + 1) * PC], v, (((1,), (1,)), ((), ())), preferred_element_type=F32
                )
                acc = jnp.where(piece_of == j, got, acc)
            total = part[...]
            for a in thirds(acc)[::-1]:
                total = total + jnp.dot(a, pick, preferred_element_type=F32)
            part[...] = total
        return run

    finish = gather(
        vbuf, SLOT, f, t, y, z, even, s1, r1, s2, r2,
        [prepare, level(0), level(1), level(2), level(3), level(4)],
    )

    tp_id = lambda p: (f, p)
    y_id = lambda p: (p * NZ + z, t)
    z_id = lambda p: (y * NZ + p, t)

    slab = lambda p: pl.ds(pl.multiple_of(p * 16, 16), 16)
    c1 = exchange(lambda p: part.at[slab(p)], lambda p: tbuf.at[p], tp_id, t, ps, pr)
    tbuf[t] = part[slab(t), :]
    arrived(lambda p: tbuf.at[p], tp_id, t, ps, pr)
    sums = tbuf[0]
    for p in range(1, 8):
        sums = sums + tbuf[p]
    proj_ref[slab(t), :] = sums
    c2 = exchange(lambda p: proj_ref.at[slab(t)], lambda p: proj_ref.at[slab(p)], tp_id, t, as_, ar)
    arrived(lambda p: proj_ref.at[slab(p)], tp_id, t, as_, ar)

    pv = proj_ref[...]
    gpart[...] = lax.dot_general(pv, pv, (((0,), (0,)), ((), ())), precision=HIGHEST, preferred_element_type=F32)
    tile = lambda p: (
        pl.ds(pl.multiple_of(t * 32 + (p // 2) * 8, 8), 8),
        pl.ds(pl.multiple_of(lax.rem(p, 2) * 128, 128), 128),
    )
    c3 = exchange(lambda p: gpart.at[tile(p)], lambda p: ybuf.at[p], y_id, y, ys, yr)
    ybuf[y] = gpart[tile(y)]

    split = thirds(pv)[:2]
    for j in range(PARTS):
        cols = slice(j * PC, (j + 1) * PC)
        total = jnp.zeros((PC, RANK), F32)
        for a in split[::-1]:
            total = total + lax.dot_general(
                b_ref[:, cols], a, (((0,), (0,)), ((), ())), preferred_element_type=F32
            )
        for i in range(16):
            work[(j * 16 + i) * PACK:(j * 16 + i + 1) * PACK, :] = pack(total[i * CUT:(i + 1) * CUT, :])
    cut = lambda ax, origin, i: pl.ds(pl.multiple_of(slot_of(ax, origin, i) * PACK, 16), PACK)
    streams = [(ax, d, i) for i in range(4) for ax in range(2) for d in range(2)]
    hops = lambda d, i: 4 if fourth(d, i) else 3
    sent = []

    def pass_on(ax, d, i, h, src):
        copy = pltpu.make_async_remote_copy(
            src_ref=src, dst_ref=land.at[ax, d, i, h], send_sem=s3.at[ax, d, i, h], recv_sem=r3.at[ax, d, i, h],
            device_id=(beside(ax, d, y, z), t), device_id_type=MESH,
        )
        copy.start()
        sent.append(copy)

    def came(ax, d, i, h):
        pltpu.make_async_remote_copy(
            src_ref=land.at[ax, d, i, h], dst_ref=land.at[ax, d, i, h], send_sem=s3.at[ax, d, i, h],
            recv_sem=r3.at[ax, d, i, h], device_id=aside, device_id_type=MESH,
        ).wait_recv()

    def ring(h):
        for ax, d, i in streams:
            n = hops(d, i)
            if h < n:
                came(ax, d, i, h)
                if h + 1 < n:
                    step = 1 if d == 0 else -1
                    own = work[cut(ax, mod8(at[ax] + step * (n - h - 1)), i), :].astype(F32)
                    land[ax, d, i, h] = (land[ax, d, i, h].astype(F32) + own).astype(BF16)
                    pass_on(ax, d, i, h + 1, land.at[ax, d, i, h])

    for ax, d, i in streams:
        step = 1 if d == 0 else -1
        pass_on(ax, d, i, 0, work.at[cut(ax, mod8(at[ax] + step * hops(d, i)), i)])
    arrived(lambda p: ybuf.at[p], y_id, y, ys, yr)
    sums = ybuf[0]
    for p in range(1, 8):
        sums = sums + ybuf[p]
    zbuf[z] = sums
    c4 = exchange(lambda p: zbuf.at[z], lambda p: zbuf.at[p], z_id, z, zs, zr)
    ring(0)
    arrived(lambda p: zbuf.at[p], z_id, z, zs, zr)
    sums = zbuf[0]
    for p in range(1, 8):
        sums = sums + zbuf[p]
    gram_ref[tile(y)] = sums
    c5 = exchange(lambda p: gram_ref.at[tile(y)], lambda p: gram_ref.at[tile(p)], y_id, y, bs, br)
    ring(1)
    arrived(lambda p: gram_ref.at[tile(p)], y_id, y, bs, br)
    block = lambda p: pl.ds(pl.multiple_of(p * 32, 32), 32)
    c6 = exchange(lambda p: gram_ref.at[block(t)], lambda p: gram_ref.at[block(p)], tp_id, t, ts, tr)
    ring(2)
    ring(3)

    spot = jnp.where(even, y, z)

    def target(ax, i):
        odd = lax.rem(at[ax], 2) if ax == 0 else 1 - lax.rem(at[ax], 2)
        return 2 * i + odd

    def cross(ax, i, device):
        return pltpu.make_async_remote_copy(
            src_ref=near.at[ax, i], dst_ref=far.at[at[1 - ax]], send_sem=s4.at[ax, i], recv_sem=r4.at[at[1 - ax]],
            device_id=device, device_id_type=MESH,
        )

    for ax in range(2):
        for i in range(4):
            both = work[cut(ax, at[ax], i), :].astype(F32)
            for d in range(2):
                both = both + land[ax, d, i, hops(d, i) - 1].astype(F32)
            near[ax, i] = both.astype(BF16)
            to = target(ax, i)

            @pl.when(to != at[1 - ax])
            def _():
                cross(ax, i, ((to * NZ + z) if ax == 0 else (y * NZ + to), t)).start()

            @pl.when(to == at[1 - ax])
            def _():
                far[at[1 - ax]] = both.astype(BF16)

    arrived(lambda p: gram_ref.at[block(p)], tp_id, t, ts, tr)
    start_inverse(gram_ref[...], sx)

    def advance(i, carry):
        step_inverse(sx)
        return carry

    lax.fori_loop(0, 5, advance, 0)
    check_ref[0] = missed(sx)
    for k in range(1, 8):
        p = mod8(spot + k)
        pltpu.make_async_remote_copy(
            src_ref=far.at[p], dst_ref=far.at[p], send_sem=s4.at[0, 0], recv_sem=r4.at[p],
            device_id=aside, device_id_type=MESH,
        ).wait_recv()
    sums = far[0].astype(F32)
    for p in range(1, 8):
        sums = sums + far[p].astype(F32)
    zown = jnp.concatenate([sums[:CUT], sums[CUT:]], axis=1)
    sems = (s5, r5, s6, r6, e1, f1, e2, f2, e3, f3)
    spread(
        zown, sx, proj_ref, check_ref, low_ref, back_ref, sq_ref, (f, t, y, z, even), q1, q2, q3, sems
    )
    finish()
    for copies in (c1, c2, c3, c4, c5, c6, sent):
        for copy in copies:
            copy.wait_send()
    for ax in range(2):
        for i in range(4):
            @pl.when(target(ax, i) != at[1 - ax])
            def _():
                cross(ax, i, aside).wait_send()


def output_kernel(b_ref, low_ref, back_ref, sq_ref, mom_ref, own_ref, upd_ref, mbuf, ubuf, sem):
    f = lax.axis_index("fsdp")
    squares = sq_ref[0:1, :] + epsilon
    inverse = lax.rsqrt(squares)
    low = low_ref[...]
    scaled = (low.astype(F32) * jnp.sqrt(squares).astype(BF16).astype(F32)).astype(BF16)
    pick = jnp.where(
        lax.broadcasted_iota(jnp.int32, (8, RANK), 0) + f * OWN == lax.broadcasted_iota(jnp.int32, (8, RANK), 1),
        1.0, 0.0,
    ).astype(BF16)
    turn = (((1,), (1,)), ((), ()))
    copies = []
    for j in range(PARTS):
        cols = slice(j * PC, (j + 1) * PC)
        halves = [
            jnp.concatenate(
                [
                    back_ref[s * PACK + h * CUT:s * PACK + (h + 1) * CUT, :].astype(F32)
                    for s in range(j * 16, (j + 1) * 16)
                ],
                axis=0,
            )
            for h in range(2)
        ]
        nb = (jnp.concatenate(halves, axis=1) * inverse).astype(BF16)
        own_ref[:, cols] = lax.dot_general(pick, nb, turn, preferred_element_type=F32)[0:OWN].astype(BF16)
        ubuf[:, cols] = (UNIT * lax.dot_general(low, nb, turn, preferred_element_type=F32)).astype(BF16)
        mbuf[:, cols] = (
            b_ref[:, cols].astype(F32)
            - (1.0 - momentum_decay) * lax.dot_general(scaled, nb, turn, preferred_element_type=F32)
        ).astype(BF16)
        for n, (src, dst) in enumerate(((ubuf, upd_ref), (mbuf, mom_ref))):
            copy = pltpu.make_async_copy(src.at[:, cols], dst.at[:, cols], sem.at[n, j])
            copy.start()
            copies.append(copy)
    for copy in copies:
        copy.wait()


VMEM = pl.BlockSpec(memory_space=pltpu.VMEM)
HBM = pl.BlockSpec(memory_space=pltpu.HBM)
DMA = pltpu.SemaphoreType.DMA
LIMIT = 44 * 2**20
WIDE = (2, 2, 4, 4)


def project(momentum, gradient, basis_rows):
    return pl.pallas_call(
        project_kernel,
        out_shape=[
            jax.ShapeDtypeStruct((ROWS, RANK), F32),
            jax.ShapeDtypeStruct((RANK, RANK), F32),
            jax.ShapeDtypeStruct((2,), F32),
            jax.ShapeDtypeStruct((ROWS, COLS), BF16),
            jax.ShapeDtypeStruct((ROWS, RANK), BF16),
            jax.ShapeDtypeStruct((NF * PACK, HALF), BF16),
            jax.ShapeDtypeStruct((8, RANK), F32),
        ],
        in_specs=[HBM, HBM, HBM],
        out_specs=[VMEM, VMEM, pl.BlockSpec(memory_space=pltpu.SMEM), VMEM, VMEM, VMEM, VMEM],
        scratch_shapes=[
            pltpu.VMEM((NF * SLOT, PC), BF16),
            pltpu.VMEM((ROWS, COLS), BF16),
            pltpu.VMEM((ROWS, COLS), BF16),
            pltpu.VMEM((OWN, COLS), BF16),
            pltpu.VMEM((NF * SLOT, RANK), BF16),
            pltpu.VMEM((ROWS, RANK), F32),
            pltpu.VMEM((8, 16, RANK), F32),
            pltpu.VMEM((RANK, RANK), F32),
            pltpu.VMEM((8, 8, 128), F32),
            pltpu.VMEM((8, 8, 128), F32),
            pltpu.VMEM((NF * PACK, HALF), BF16),
            pltpu.VMEM(WIDE + (PACK, HALF), BF16),
            pltpu.VMEM((2, 4, PACK, HALF), BF16),
            pltpu.VMEM((8, PACK, HALF), BF16),
            pltpu.VMEM((RANK, 2 * RANK), F32),
            pltpu.VMEM((8, 8, RANK), F32),
            pltpu.VMEM((8, 8, RANK), F32),
            pltpu.VMEM((8, 8, RANK), F32),
            DMA((3,)),
            DMA((8,)), DMA((8,)), DMA(WIDE), DMA(WIDE), DMA(WIDE), DMA(WIDE), DMA((2, 4)), DMA((8,)),
            DMA((8,)), DMA((8,)), DMA(WIDE), DMA(WIDE),
        ] + [DMA((8,))] * 18,
        compiler_params=pltpu.CompilerParams(collective_id=0, has_side_effects=True, vmem_limit_bytes=LIMIT),
        name="project",
    )(momentum, gradient, basis_rows)


def outputs(buffer, low, back, squares):
    return pl.pallas_call(
        output_kernel,
        out_shape=[
            jax.ShapeDtypeStruct((ROWS, COLS), BF16),
            jax.ShapeDtypeStruct((OWN, COLS), BF16),
            jax.ShapeDtypeStruct((ROWS, COLS), BF16),
        ],
        in_specs=[VMEM] * 4,
        out_specs=[HBM, VMEM, HBM],
        scratch_shapes=[pltpu.VMEM((ROWS, COLS), BF16)] * 2 + [DMA((2, PARTS))],
        compiler_params=pltpu.CompilerParams(vmem_limit_bytes=32 * 2**20),
        name="outputs",
    )(buffer, low, back, squares)


def direct(proj, gram, buffer):
    lower_factor = jnp.linalg.cholesky(gram)
    low = lax.linalg.triangular_solve(
        lower_factor, proj, left_side=False, lower=True, transpose_a=True
    ).astype(BF16)
    back = lax.psum(
        lax.dot_general(low, buffer, (((0,), (0,)), ((), ())), preferred_element_type=F32), "fsdp"
    )
    squares = lax.psum(jnp.sum(back * back, axis=1), "tp")
    packed = back.T.reshape(NF, CUT, 2, HALF).transpose(0, 2, 1, 3).reshape(NF * PACK, HALF)
    return low, packed.astype(BF16), jnp.broadcast_to(squares[None, :], (8, RANK))


def local(momentum, gradient, basis_rows):
    proj, gram, check, buffer, low, back, squares = project(momentum, gradient, basis_rows)
    return lax.cond(
        jnp.logical_and(check[0] < 1e-8, check[1] < 4.0),
        lambda proj, gram, buffer, *now: tuple(outputs(buffer, *now)),
        lambda proj, gram, buffer, *now: tuple(outputs(buffer, *direct(proj, gram, buffer))),
        proj, gram, buffer, low, back, squares,
    )


def solution(mesh):
    return jax.shard_map(
        local,
        mesh=mesh,
        in_specs=(P("fsdp", "tp"), P("fsdp", "tp"), P("fsdp", "tp")),
        out_specs=(P("fsdp", "tp"), P("fsdp", "tp"), P("fsdp", "tp")),
        check_vma=False,
    )
```

```python
import functools
import math

import jax
import jax.numpy as jnp
from jax import lax
from jax.experimental import pallas as pl
from jax.experimental.pallas import tpu as pltpu
from jax.sharding import PartitionSpec as P

D = 8192
FF = 28672
RANK = 256
NY = 8
NZ = 8
NF = 64
NT = 8
ROWS = D // NF
COLS = FF // NT
OWN = RANK // NF
PARTS = 4
PC = COLS // PARTS
SLOT = 16
CUT = COLS // NF
PACK = 2 * CUT
HALF = RANK // 2

epsilon = 1e-06
momentum_decay = 0.95
UNIT = math.sqrt(D * FF / RANK)

F32 = jnp.float32
BF16 = jnp.bfloat16
MESH = pl.DeviceIdType.MESH
HIGHEST = lax.Precision.HIGHEST


def mod8(v):
    return lax.rem(v + 16, 8)


def place():
    f = lax.axis_index("fsdp")
    t = lax.axis_index("tp")
    y = f // NZ
    z = lax.rem(f, NZ)
    even = lax.rem(y + z, 2) == 0
    return f, t, y, z, even


def line(even, y, z, k):
    along_y = jnp.where(even, k, 0)
    along_z = jnp.where(even, 0, k)
    return mod8(y + along_y) * NZ + mod8(z + along_z)


def own_slot(even, y, z):
    return jnp.where(even, z * 4 + y // 2, 32 + y * 4 + z // 2)


def greet(f, t, y, z):
    barrier = pltpu.get_barrier_semaphore()
    for k in range(1, 8):
        pl.semaphore_signal(barrier, inc=1, device_id=(mod8(y + k) * NZ + z, t), device_id_type=MESH)
        pl.semaphore_signal(barrier, inc=1, device_id=(y * NZ + mod8(z + k), t), device_id_type=MESH)
        pl.semaphore_signal(barrier, inc=1, device_id=(f, mod8(t + k)), device_id_type=MESH)


def met():
    pl.semaphore_wait(pltpu.get_barrier_semaphore(), 21)


WAVE = (
    (0, None), (1, None), (3, None), (0, 0), (2, None), (1, 0), (3, 0), (0, 1), (2, 0), (1, 1), (3, 1), (0, 2),
    (2, 1), (1, 2), (3, 2), (0, 3), (2, 2), (1, 3), (3, 3), (2, 3),
)


def fourth(d, i):
    return (i < 2) if d == 0 else (i >= 2)


def slot_of(ax, origin, i):
    return ax * 32 + origin * 4 + i


def beside(ax, d, y, z):
    step = 1 if d == 0 else -1
    return (y * NZ + mod8(z + step)) if ax == 0 else (mod8(y + step) * NZ + z)


def gather(buf, size, f, t, y, z, even, s1, r1, s2, r2, between):
    rows = lambda slot: buf.at[pl.ds(pl.multiple_of(slot * size, size), size)]
    me = own_slot(even, y, z)
    at = (z, y)
    half = (y // 2, z // 2)
    home = (even, jnp.logical_not(even))
    here = jnp.where(even, y // 2, 4 + z // 2)
    aside = (f, mod8(t + 1))

    def straight(k, to):
        return pltpu.make_async_remote_copy(
            src_ref=rows(me), dst_ref=rows(me), send_sem=s1.at[k], recv_sem=r1.at[here],
            device_id=to, device_id_type=MESH,
        )

    def copy(ax, d, i, h, origin, to):
        slot = slot_of(ax, origin, i)
        return pltpu.make_async_remote_copy(
            src_ref=rows(slot), dst_ref=rows(slot), send_sem=s2.at[ax, d, i, h], recv_sem=r2.at[ax, d, i, h],
            device_id=to, device_id_type=MESH,
        )

    def send(ax, d, i, h):
        step = 1 if d == 0 else -1
        copy(ax, d, i, h, mod8(at[ax] - step * h), (beside(ax, d, y, z), t)).start()

    def landed(ax, d, i, h):
        step = 1 if d == 0 else -1
        copy(ax, d, i, h, mod8(at[ax] - step * (h + 1)), aside).wait_recv()

    for ax in range(2):
        @pl.when(home[ax])
        def _():
            for d in range(2):
                send(ax, d, half[ax], 0)
    for k in (1, 7, 2, 6, 3, 5, 4):
        straight(k, (line(even, y, z, k), t)).start()
    between[0]()
    for r, h in WAVE:
        for ax in range(2):
            i = lax.rem(half[ax] + r, 4)

            def first():
                slot = slot_of(ax, at[ax], i)
                pltpu.make_async_remote_copy(
                    src_ref=rows(slot), dst_ref=rows(slot), send_sem=s1.at[0], recv_sem=r1.at[ax * 4 + i],
                    device_id=aside, device_id_type=MESH,
                ).wait_recv()
                for d in range(2):
                    send(ax, d, i, 0)

            if h is None:
                if r == 0:
                    pl.when(jnp.logical_not(home[ax]))(first)
                else:
                    first()
                continue
            for d in range(2):
                if h < 2:
                    landed(ax, d, i, h)
                    send(ax, d, i, h + 1)
                elif h == 2:
                    landed(ax, d, i, h)

                    @pl.when(fourth(d, i))
                    def _():
                        send(ax, d, i, 3)
                else:

                    @pl.when(fourth(d, i))
                    def _():
                        landed(ax, d, i, 3)
        if r == 2:
            between[1 if h is None else h + 2]()

    def finish():
        for k in range(1, 8):
            straight(k, aside).wait_send()
        for ax in range(2):
            for d in range(2):
                for i in range(4):
                    for h in range(4 if fourth(d, i) else 3):
                        copy(ax, d, i, h, at[ax], aside).wait_send()

    return finish


def exchange(src_of, dst_of, ids, pos, send, recv):
    copies = []
    for k in (4, 3, 5, 2, 6, 1, 7):
        p = mod8(pos + k)
        copy = pltpu.make_async_remote_copy(
            src_ref=src_of(p),
            dst_ref=dst_of(pos),
            send_sem=send.at[k],
            recv_sem=recv.at[8 - k],
            device_id=ids(p),
            device_id_type=MESH,
        )
        copy.start()
        copies.append(copy)
    return copies


def arrived(dst_of, ids, pos, send, recv):
    for k in range(1, 8):
        p = mod8(pos + k)
        pltpu.make_async_remote_copy(
            src_ref=dst_of(p),
            dst_ref=dst_of(p),
            send_sem=send.at[k],
            recv_sem=recv.at[k],
            device_id=ids(p),
            device_id_type=MESH,
        ).wait_recv()


def start_inverse(gram, sx):
    i = lax.broadcasted_iota(jnp.int32, (RANK, RANK), 0)
    j = lax.broadcasted_iota(jnp.int32, (RANK, RANK), 1)
    on = jnp.where(i == j, gram, 0.0)
    down = lax.rsqrt(jnp.sum(on, axis=1, keepdims=True))
    across = lax.rsqrt(jnp.sum(on, axis=0, keepdims=True))
    sx[:, :RANK] = gram * down * across
    sx[:, RANK:] = jnp.where(i == j, down, 0.0)


def step_inverse(sx):
    i = lax.broadcasted_iota(jnp.int32, (RANK, RANK), 0)
    j = lax.broadcasted_iota(jnp.int32, (RANK, RANK), 1)
    e = sx[:, :RANK] - jnp.where(i == j, 1.0, 0.0)
    w = jnp.where(i > j, -e, jnp.where(i == j, 1.0 - 0.5 * e, 0.0))
    out = jnp.dot(w, sx[...], precision=HIGHEST, preferred_element_type=F32)
    sx[:, RANK:] = out[:, RANK:]
    sx[:, :RANK] = lax.dot_general(
        out[:, :RANK], w, (((1,), (1,)), ((), ())), precision=HIGHEST, preferred_element_type=F32
    )


def missed(sx):
    i = lax.broadcasted_iota(jnp.int32, (RANK, RANK), 0)
    j = lax.broadcasted_iota(jnp.int32, (RANK, RANK), 1)
    e = sx[:, :RANK] - jnp.where(i == j, 1.0, 0.0)
    return jnp.sum(e * e)


def pack(columns):
    return jnp.concatenate([columns[:, :HALF], columns[:, HALF:]], axis=0).astype(BF16)


def spread(zown, sx, proj_ref, check_ref, low_ref, back_ref, sq_ref, where, q1, q2, q3, sems):
    f, t, y, z, even = where
    s1, r1, s2, r2, e1, f1, e2, f2, e3, f3 = sems
    me = own_slot(even, y, z)
    tp_id = lambda p: (f, p)
    y_id = lambda p: (p * NZ + z, t)
    z_id = lambda p: (y * NZ + p, t)
    turn = (((1,), (1,)), ((), ()))
    mine = lax.dot_general(zown, sx[:, RANK:], turn, precision=HIGHEST, preferred_element_type=F32)
    back_ref[pl.ds(pl.multiple_of(me * PACK, 16), PACK), :] = pack(mine)
    first = lax.broadcasted_iota(jnp.int32, (8, RANK), 0) == 0
    q1[t] = jnp.where(
        first, jnp.sum(mine * mine, axis=0, keepdims=True), jnp.sum(zown * zown, axis=0, keepdims=True)
    )
    waits = []

    def open_squares():
        waits.extend(exchange(lambda p: q1.at[t], lambda p: q1.at[p], tp_id, t, e1, f1))
        low_ref[...] = lax.dot_general(
            proj_ref[...], sx[:, RANK:], turn, precision=HIGHEST, preferred_element_type=F32
        ).astype(BF16)

    def fold(buf):
        sums = buf[0]
        for p in range(1, 8):
            sums = sums + buf[p]
        return sums

    def over_y():
        arrived(lambda p: q1.at[p], tp_id, t, e1, f1)
        q2[y] = fold(q1)
        waits.extend(exchange(lambda p: q2.at[y], lambda p: q2.at[p], y_id, y, e2, f2))

    def over_z():
        arrived(lambda p: q2.at[p], y_id, y, e2, f2)
        q3[z] = fold(q2)
        waits.extend(exchange(lambda p: q3.at[z], lambda p: q3.at[p], z_id, z, e3, f3))

    nothing = lambda: None
    finish = gather(
        back_ref, PACK, f, t, y, z, even, s1, r1, s2, r2,
        [open_squares, over_y, over_z, nothing, nothing, nothing],
    )
    arrived(lambda p: q3.at[p], z_id, z, e3, f3)
    squares = fold(q3)
    sq_ref[...] = squares
    x = sx[:, RANK:]
    grown = lax.dot_general(squares, x * x, turn, precision=HIGHEST, preferred_element_type=F32)[1:2, :]
    check_ref[1] = jnp.sum(grown / squares[0:1, :]) * (1.0 / RANK)
    finish()
    for copy in waits:
        copy.wait_send()


def thirds(v):
    a1 = v.astype(BF16)
    rest = v - a1.astype(F32)
    a2 = rest.astype(BF16)
    return a1, a2, (rest - a2.astype(F32)).astype(BF16)


def project_kernel(
    m_ref, g_ref, basis_ref, proj_ref, gram_ref, check_ref, b_ref, low_ref, back_ref, sq_ref,
    vbuf, mbuf, gbuf, stage, sel, part, tbuf, gpart, ybuf, zbuf, work, land, near, far, sx, q1, q2, q3,
    local_sem, s1, r1, s2, r2, s3, r3, s4, r4, s5, r5, s6, r6, ps, pr, as_, ar, ys, yr, zs, zr, bs, br, ts, tr,
    e1, f1, e2, f2, e3, f3,
):
    f, t, y, z, even = place()
    me = own_slot(even, y, z)
    at = (z, y)
    aside = (f, mod8(t + 1))
    cm = pltpu.make_async_copy(m_ref, mbuf, local_sem.at[0])
    cg = pltpu.make_async_copy(g_ref, gbuf, local_sem.at[1])
    cb = pltpu.make_async_copy(basis_ref, stage, local_sem.at[2])
    cb.start()
    cm.start()
    cg.start()
    greet(f, t, y, z)
    cb.wait()
    own = stage[...].astype(F32)
    pieces = [own[:, j * PC:(j + 1) * PC] for j in range(PARTS)]
    vbuf[pl.ds(pl.multiple_of(me * SLOT, SLOT), SLOT), :] = jnp.concatenate(pieces, axis=0).astype(BF16)
    met()

    def prepare():
        cm.wait()
        cg.wait()
        for j in range(PARTS):
            cols = slice(j * PC, (j + 1) * PC)
            b_ref[:, cols] = (mbuf[:, cols].astype(F32) + gbuf[:, cols].astype(F32)).astype(BF16)
        part[...] = jnp.zeros((ROWS, RANK), F32)

        def choose(i, carry):
            base = pl.multiple_of(i * 128, 128)
            row = base + lax.broadcasted_iota(jnp.int32, (128, RANK), 0)
            slot = row // SLOT
            first, second = (slot // 4) % 8, slot % 4
            yf = 2 * second + (first % 2)
            zo = 2 * second + (1 - first % 2)
            dev = jnp.where(slot < 32, yf * NZ + first, first * NZ + zo)
            hit = dev * OWN + row % 4 == lax.broadcasted_iota(jnp.int32, (128, RANK), 1)
            sel[pl.ds(base, 128), :] = jnp.where(hit, 1.0, 0.0).astype(BF16)
            return carry

        lax.fori_loop(0, 8, choose, 0)

    def level(h):
        def run():
            if h == 0 or h == 4:
                starts = [slot_of(ax, mod8(at[ax] + h), 0) * SLOT for ax in range(2)]
            else:
                starts = [slot_of(ax, mod8(at[ax] + s), 0) * SLOT for ax in range(2) for s in (h, -h)]
            spans = [pl.ds(pl.multiple_of(s, 64), 64) for s in starts]
            v = jnp.concatenate([vbuf[s, :] for s in spans], axis=0)
            pick = jnp.concatenate([sel[s, :] for s in spans], axis=0)
            piece_of = (lax.broadcasted_iota(jnp.int32, (ROWS, v.shape[0]), 1) // 4) % 4
            acc = jnp.zeros((ROWS, v.shape[0]), F32)
            for j in range(PARTS):
                got = lax.dot_general(
                    b_ref[:, j * PC:(j + 1) * PC], v, (((1,), (1,)), ((), ())), preferred_element_type=F32
                )
                acc = jnp.where(piece_of == j, got, acc)
            total = part[...]
            for a in thirds(acc)[::-1]:
                total = total + jnp.dot(a, pick, preferred_element_type=F32)
            part[...] = total
        return run

    finish = gather(
        vbuf, SLOT, f, t, y, z, even, s1, r1, s2, r2,
        [prepare, level(0), level(1), level(2), level(3), level(4)],
    )

    tp_id = lambda p: (f, p)
    y_id = lambda p: (p * NZ + z, t)
    z_id = lambda p: (y * NZ + p, t)

    slab = lambda p: pl.ds(pl.multiple_of(p * 16, 16), 16)
    c1 = exchange(lambda p: part.at[slab(p)], lambda p: tbuf.at[p], tp_id, t, ps, pr)
    tbuf[t] = part[slab(t), :]
    arrived(lambda p: tbuf.at[p], tp_id, t, ps, pr)
    sums = tbuf[0]
    for p in range(1, 8):
        sums = sums + tbuf[p]
    proj_ref[slab(t), :] = sums
    c2 = exchange(lambda p: proj_ref.at[slab(t)], lambda p: proj_ref.at[slab(p)], tp_id, t, as_, ar)
    arrived(lambda p: proj_ref.at[slab(p)], tp_id, t, as_, ar)

    pv = proj_ref[...]
    gpart[...] = lax.dot_general(pv, pv, (((0,), (0,)), ((), ())), precision=HIGHEST, preferred_element_type=F32)
    tile = lambda p: (
        pl.ds(pl.multiple_of(t * 32 + (p // 2) * 8, 8), 8),
        pl.ds(pl.multiple_of(lax.rem(p, 2) * 128, 128), 128),
    )
    c3 = exchange(lambda p: gpart.at[tile(p)], lambda p: ybuf.at[p], y_id, y, ys, yr)
    ybuf[y] = gpart[tile(y)]

    split = thirds(pv)[:2]
    for j in range(PARTS):
        cols = slice(j * PC, (j + 1) * PC)
        total = jnp.zeros((PC, RANK), F32)
        for a in split[::-1]:
            total = total + lax.dot_general(
                b_ref[:, cols], a, (((0,), (0,)), ((), ())), preferred_element_type=F32
            )
        for i in range(16):
            work[(j * 16 + i) * PACK:(j * 16 + i + 1) * PACK, :] = pack(total[i * CUT:(i + 1) * CUT, :])
    cut = lambda ax, origin, i: pl.ds(pl.multiple_of(slot_of(ax, origin, i) * PACK, 16), PACK)
    streams = [(ax, d, i) for i in range(4) for ax in range(2) for d in range(2)]
    hops = lambda d, i: 4 if fourth(d, i) else 3
    sent = []

    def pass_on(ax, d, i, h, src):
        copy = pltpu.make_async_remote_copy(
            src_ref=src, dst_ref=land.at[ax, d, i, h], send_sem=s3.at[ax, d, i, h], recv_sem=r3.at[ax, d, i, h],
            device_id=(beside(ax, d, y, z), t), device_id_type=MESH,
        )
        copy.start()
        sent.append(copy)

    def came(ax, d, i, h):
        pltpu.make_async_remote_copy(
            src_ref=land.at[ax, d, i, h], dst_ref=land.at[ax, d, i, h], send_sem=s3.at[ax, d, i, h],
            recv_sem=r3.at[ax, d, i, h], device_id=aside, device_id_type=MESH,
        ).wait_recv()

    def ring(h):
        for ax, d, i in streams:
            n = hops(d, i)
            if h < n:
                came(ax, d, i, h)
                if h + 1 < n:
                    step = 1 if d == 0 else -1
                    own = work[cut(ax, mod8(at[ax] + step * (n - h - 1)), i), :].astype(F32)
                    land[ax, d, i, h] = (land[ax, d, i, h].astype(F32) + own).astype(BF16)
                    pass_on(ax, d, i, h + 1, land.at[ax, d, i, h])

    for ax, d, i in streams:
        step = 1 if d == 0 else -1
        pass_on(ax, d, i, 0, work.at[cut(ax, mod8(at[ax] + step * hops(d, i)), i)])
    arrived(lambda p: ybuf.at[p], y_id, y, ys, yr)
    sums = ybuf[0]
    for p in range(1, 8):
        sums = sums + ybuf[p]
    zbuf[z] = sums
    c4 = exchange(lambda p: zbuf.at[z], lambda p: zbuf.at[p], z_id, z, zs, zr)
    ring(0)
    arrived(lambda p: zbuf.at[p], z_id, z, zs, zr)
    sums = zbuf[0]
    for p in range(1, 8):
        sums = sums + zbuf[p]
    gram_ref[tile(y)] = sums
    c5 = exchange(lambda p: gram_ref.at[tile(y)], lambda p: gram_ref.at[tile(p)], y_id, y, bs, br)
    ring(1)
    arrived(lambda p: gram_ref.at[tile(p)], y_id, y, bs, br)
    block = lambda p: pl.ds(pl.multiple_of(p * 32, 32), 32)
    c6 = exchange(lambda p: gram_ref.at[block(t)], lambda p: gram_ref.at[block(p)], tp_id, t, ts, tr)
    ring(2)
    ring(3)

    spot = jnp.where(even, y, z)

    def target(ax, i):
        odd = lax.rem(at[ax], 2) if ax == 0 else 1 - lax.rem(at[ax], 2)
        return 2 * i + odd

    def cross(ax, i, device):
        return pltpu.make_async_remote_copy(
            src_ref=near.at[ax, i], dst_ref=far.at[at[1 - ax]], send_sem=s4.at[ax, i], recv_sem=r4.at[at[1 - ax]],
            device_id=device, device_id_type=MESH,
        )

    for ax in range(2):
        for i in range(4):
            both = work[cut(ax, at[ax], i), :].astype(F32)
            for d in range(2):
                both = both + land[ax, d, i, hops(d, i) - 1].astype(F32)
            near[ax, i] = both.astype(BF16)
            to = target(ax, i)

            @pl.when(to != at[1 - ax])
            def _():
                cross(ax, i, ((to * NZ + z) if ax == 0 else (y * NZ + to), t)).start()

            @pl.when(to == at[1 - ax])
            def _():
                far[at[1 - ax]] = both.astype(BF16)

    arrived(lambda p: gram_ref.at[block(p)], tp_id, t, ts, tr)
    start_inverse(gram_ref[...], sx)

    def advance(i, carry):
        step_inverse(sx)
        return carry

    lax.fori_loop(0, 5, advance, 0)
    check_ref[0] = missed(sx)
    for k in range(1, 8):
        p = mod8(spot + k)
        pltpu.make_async_remote_copy(
            src_ref=far.at[p], dst_ref=far.at[p], send_sem=s4.at[0, 0], recv_sem=r4.at[p],
            device_id=aside, device_id_type=MESH,
        ).wait_recv()
    sums = far[0].astype(F32)
    for p in range(1, 8):
        sums = sums + far[p].astype(F32)
    zown = jnp.concatenate([sums[:CUT], sums[CUT:]], axis=1)
    sems = (s5, r5, s6, r6, e1, f1, e2, f2, e3, f3)
    spread(
        zown, sx, proj_ref, check_ref, low_ref, back_ref, sq_ref, (f, t, y, z, even), q1, q2, q3, sems
    )
    finish()
    for copies in (c1, c2, c3, c4, c5, c6, sent):
        for copy in copies:
            copy.wait_send()
    for ax in range(2):
        for i in range(4):
            @pl.when(target(ax, i) != at[1 - ax])
            def _():
                cross(ax, i, aside).wait_send()


def output_kernel(b_ref, low_ref, back_ref, sq_ref, mom_ref, own_ref, upd_ref, mbuf, ubuf, sem):
    f = lax.axis_index("fsdp")
    squares = sq_ref[0:1, :] + epsilon
    inverse = lax.rsqrt(squares)
    low = low_ref[...]
    scaled = (low.astype(F32) * jnp.sqrt(squares).astype(BF16).astype(F32)).astype(BF16)
    pick = jnp.where(
        lax.broadcasted_iota(jnp.int32, (8, RANK), 0) + f * OWN == lax.broadcasted_iota(jnp.int32, (8, RANK), 1),
        1.0, 0.0,
    ).astype(BF16)
    turn = (((1,), (1,)), ((), ()))
    copies = []
    for j in range(PARTS):
        cols = slice(j * PC, (j + 1) * PC)
        halves = [
            jnp.concatenate(
                [
                    back_ref[s * PACK + h * CUT:s * PACK + (h + 1) * CUT, :].astype(F32)
                    for s in range(j * 16, (j + 1) * 16)
                ],
                axis=0,
            )
            for h in range(2)
        ]
        nb = (jnp.concatenate(halves, axis=1) * inverse).astype(BF16)
        own_ref[:, cols] = lax.dot_general(pick, nb, turn, preferred_element_type=F32)[0:OWN].astype(BF16)
        ubuf[:, cols] = (UNIT * lax.dot_general(low, nb, turn, preferred_element_type=F32)).astype(BF16)
        mbuf[:, cols] = (
            b_ref[:, cols].astype(F32)
            - (1.0 - momentum_decay) * lax.dot_general(scaled, nb, turn, preferred_element_type=F32)
        ).astype(BF16)
        for n, (src, dst) in enumerate(((ubuf, upd_ref), (mbuf, mom_ref))):
            copy = pltpu.make_async_copy(src.at[:, cols], dst.at[:, cols], sem.at[n, j])
            copy.start()
            copies.append(copy)
    for copy in copies:
        copy.wait()


VMEM = pl.BlockSpec(memory_space=pltpu.VMEM)
HBM = pl.BlockSpec(memory_space=pltpu.HBM)
DMA = pltpu.SemaphoreType.DMA
LIMIT = 56 * 2**20
WIDE = (2, 2, 4, 4)


def project(momentum, gradient, basis_rows):
    return pl.pallas_call(
        project_kernel,
        out_shape=[
            jax.ShapeDtypeStruct((ROWS, RANK), F32),
            jax.ShapeDtypeStruct((RANK, RANK), F32),
            jax.ShapeDtypeStruct((2,), F32),
            jax.ShapeDtypeStruct((ROWS, COLS), BF16),
            jax.ShapeDtypeStruct((ROWS, RANK), BF16),
            jax.ShapeDtypeStruct((NF * PACK, HALF), BF16),
            jax.ShapeDtypeStruct((8, RANK), F32),
        ],
        in_specs=[HBM, HBM, HBM],
        out_specs=[VMEM, VMEM, pl.BlockSpec(memory_space=pltpu.SMEM), VMEM, VMEM, VMEM, VMEM],
        scratch_shapes=[
            pltpu.VMEM((NF * SLOT, PC), BF16),
            pltpu.VMEM((ROWS, COLS), BF16),
            pltpu.VMEM((ROWS, COLS), BF16),
            pltpu.VMEM((OWN, COLS), BF16),
            pltpu.VMEM((NF * SLOT, RANK), BF16),
            pltpu.VMEM((ROWS, RANK), F32),
            pltpu.VMEM((8, 16, RANK), F32),
            pltpu.VMEM((RANK, RANK), F32),
            pltpu.VMEM((8, 8, 128), F32),
            pltpu.VMEM((8, 8, 128), F32),
            pltpu.VMEM((NF * PACK, HALF), BF16),
            pltpu.VMEM(WIDE + (PACK, HALF), BF16),
            pltpu.VMEM((2, 4, PACK, HALF), BF16),
            pltpu.VMEM((8, PACK, HALF), BF16),
            pltpu.VMEM((RANK, 2 * RANK), F32),
            pltpu.VMEM((8, 8, RANK), F32),
            pltpu.VMEM((8, 8, RANK), F32),
            pltpu.VMEM((8, 8, RANK), F32),
            DMA((3,)),
            DMA((8,)), DMA((8,)), DMA(WIDE), DMA(WIDE), DMA(WIDE), DMA(WIDE), DMA((2, 4)), DMA((8,)),
            DMA((8,)), DMA((8,)), DMA(WIDE), DMA(WIDE),
        ] + [DMA((8,))] * 18,
        compiler_params=pltpu.CompilerParams(collective_id=0, has_side_effects=True, vmem_limit_bytes=LIMIT),
        name="project",
    )(momentum, gradient, basis_rows)


def outputs(buffer, low, back, squares):
    return pl.pallas_call(
        output_kernel,
        out_shape=[
            jax.ShapeDtypeStruct((ROWS, COLS), BF16),
            jax.ShapeDtypeStruct((OWN, COLS), BF16),
            jax.ShapeDtypeStruct((ROWS, COLS), BF16),
        ],
        in_specs=[VMEM] * 4,
        out_specs=[HBM, VMEM, HBM],
        scratch_shapes=[pltpu.VMEM((ROWS, COLS), BF16)] * 2 + [DMA((2, PARTS))],
        compiler_params=pltpu.CompilerParams(vmem_limit_bytes=32 * 2**20),
        name="outputs",
    )(buffer, low, back, squares)


def ring_sum(value, axis, n):
    def step(_, state):
        moving, total = state
        moving = lax.ppermute(moving, axis, [(i, (i + 1) % n) for i in range(n)])
        return moving, total + moving

    return lax.fori_loop(0, n - 1, step, (value, value))[1]


def direct(proj, gram, buffer):
    lower_factor = jnp.linalg.cholesky(gram)
    low = lax.linalg.triangular_solve(
        lower_factor, proj, left_side=False, lower=True, transpose_a=True
    ).astype(BF16)
    partial = lax.dot_general(low, buffer, (((0,), (0,)), ((), ())), preferred_element_type=F32)
    back = ring_sum(partial, "fsdp", NF)
    squares = ring_sum(jnp.sum(back * back, axis=1), "tp", NT)
    packed = back.T.reshape(NF, CUT, 2, HALF).transpose(0, 2, 1, 3).reshape(NF * PACK, HALF)
    return low, packed.astype(BF16), jnp.broadcast_to(squares[None, :], (8, RANK))


def local(momentum, gradient, basis_rows):
    proj, gram, check, buffer, low, back, squares = project(momentum, gradient, basis_rows)
    return lax.cond(
        jnp.logical_and(check[0] < 1e-8, check[1] < 4.0),
        lambda proj, gram, buffer, *now: tuple(outputs(buffer, *now)),
        lambda proj, gram, buffer, *now: tuple(outputs(buffer, *direct(proj, gram, buffer))),
        proj, gram, buffer, low, back, squares,
    )


def solution(mesh):
    return jax.shard_map(
        local,
        mesh=mesh,
        in_specs=(P("fsdp", "tp"), P("fsdp", "tp"), P("fsdp", "tp")),
        out_specs=(P("fsdp", "tp"), P("fsdp", "tp"), P("fsdp", "tp")),
        check_vma=False,
    )
```
